128 devices in a mesh: ctx: 32 (over z, x, y_lo), tp: 4 (over y_hi, core).
Axes of the slice: x: 4, y: 4 (y_hi: 2, y_lo: 2; y = y_hi * 2 + y_lo), z: 4, core: 2. Of those that a mesh axis runs over, the one named last changes fastest.
Arguments:
- hidden: bfloat16 [12288, 5376], P('ctx', 'tp'), may hold values from -6 to 6
- attn_gain: float32 [5376], replicated, may hold values from 0.5 to 1.5
- w_query: bfloat16 [5376, 2048], P('ctx', 'tp')
- w_key: bfloat16 [5376, 1024], P('ctx', 'tp')
- w_value: bfloat16 [5376, 1024], P('ctx', 'tp'), may hold values from -0.078125 to 0.078125
- w_out: bfloat16 [2048, 5376], P('tp', 'ctx'), may hold values from -0.125 to 0.125
- q_gain: float32 [128], replicated, as said below
- k_gain: float32 [128], replicated
- post_gain: float32 [5376], replicated, may hold values from 0.5 to 1.5
- final_gain: float32 [5376], replicated, as said below
- lm_head: bfloat16 [8192, 5376], P('tp')
- targets: int32 [12288], P('ctx'), may hold values from 0 to 8191
- positions: int32 [12288], P('ctx'), may hold values from 0 to 65535, as said below
Outputs:
- logprobs: float32 [12288], P('ctx')
- layer_out: bfloat16 [12288, 5376], P('ctx', 'tp')
The draws below stay inside these ranges and needn't reach their ends.
Inputs may be any that keep to these rules, and one draw needn't show every extreme that they name: `positions`: along the 12288 tokens each position is one more than the one before, except at up to three document starts where it is 0, all within the last quarter of the tokens; the first document's last position is 65535. `q_gain`: query and key norms' gains are positive. `final_gain`: Positive.
All inputs are finite; a program needn't handle non-finite values.
Results may differ from the reference program's by a relative error of at most 0.015.
Values may be sent and summed in bfloat16 or wider, within the bound.
No kernel may reach another device: no remote copies, remote signals or barrier semaphores. Data moves between devices by JAX's collectives and lax.ppermute only.
A program may use at most 256 MiB of HBM per device.

```python
import math
import jax
import jax.numpy as jnp
from jax import lax

D = 5376
HEADS = 16
KV_HEADS = 8
HEAD_DIM = 128
TOKENS = 12288
VOCAB = 8192


def query_matrix(key):
    return jax.random.normal(key, (D, HEADS * HEAD_DIM), jnp.float32) * D ** (-0.5)


def draw_w_query(key, part):
    shared = query_matrix(key)
    return shared.astype(jnp.bfloat16)


def draw_w_key(key, part):
    key = jax.random.fold_in(key, 11)
    fresh = jax.random.normal(key, (D, KV_HEADS * HEAD_DIM), jnp.float32) * D ** (-0.5)
    return fresh.astype(jnp.bfloat16)


def gain_values(key, low, high):
    return jnp.exp(jax.random.uniform(key, (HEAD_DIM,), jnp.float32, jnp.log(low), jnp.log(high)))


def draw_q_gain(key, part):
    key = jax.random.fold_in(key, 21)
    return gain_values(key, 0.6, 1.5)


def draw_k_gain(key, part):
    key = jax.random.fold_in(key, 22)
    return gain_values(key, 0.6, 1.5)


def draw_final_gain(key, part):
    key = jax.random.fold_in(key, 23)
    return jax.random.uniform(key, (D,), jnp.float32, 0.7, 1.3)


def draw_lm_head(key, part):
    key = jax.random.fold_in(key, 24)
    scale_key, entry_key = jax.random.split(key)
    row_scale = jnp.exp(jax.random.uniform(scale_key, (VOCAB, 1), jnp.float32, 0.0, jnp.log(10.0)))
    entries = jax.random.normal(entry_key, (VOCAB, D), jnp.float32)
    return (entries * row_scale * D ** (-0.5)).astype(jnp.bfloat16)


def draw_positions(key, part):
    key = jax.random.fold_in(key, 25)
    lowest = 3 * TOKENS // 4
    bounds = jax.random.randint(key, (3,), lowest, TOKENS, jnp.int32)
    starts = jnp.concatenate([jnp.zeros((1,), jnp.int32), bounds])
    first_length = jnp.min(bounds)
    offset = 65536 - first_length
    token_index = jnp.arange(TOKENS, dtype=jnp.int32)
    doc_start = jnp.max(jnp.where(starts[None, :] <= token_index[:, None], starts[None, :], 0), axis=1)
    return token_index - doc_start + jnp.where(doc_start == 0, offset, 0)


def touch_ends(values, rng, low, top_value):
    index_at = [jax.random.randint(jax.random.fold_in(rng, axis), (), 0, length) for axis, length in enumerate(values.shape)]
    widest = values.shape.index(max(values.shape))
    next_to = index_at[:widest] + [(index_at[widest] + 1) % values.shape[widest]] + index_at[widest + 1:]
    return values.at[tuple(index_at)].set(low).at[tuple(next_to)].set(top_value)


def block_levels(rng, dims, pieces, low, high):
    def one(axis_at, parts):
        steps = jax.random.uniform(jax.random.fold_in(jax.random.fold_in(rng, 6), axis_at), (parts,), jnp.float32, low / len(pieces), high / len(pieces))
        return jnp.repeat(jnp.exp(steps), dims[axis_at] // parts).reshape((-1,) + (1,) * (len(dims) - axis_at - 1))

    level = one(*pieces[0])
    for cut in pieces[1:]:
        level = level * one(*cut)
    return level


def normal_values(stream_key, extent, deviation, reach, cuts=(), kind=jnp.bfloat16):
    factor_of = block_levels(stream_key, extent, cuts, -0.22, 0.18) if cuts else 1.0
    array = jax.random.normal(stream_key, extent, jnp.float32) * deviation * factor_of
    return jnp.minimum(jnp.maximum(array, -reach), reach).astype(kind)


def setup_inputs(seed: int = 0) -> dict:
    key_of = jax.random.split(jax.random.key(seed), 14)
    return {
        "hidden": normal_values(key_of[0], (TOKENS, D), 1.0, 6.0, ((0, 32), (1, 4))),
        "attn_gain": jnp.clip(1.0 + 0.1 * jax.random.normal(key_of[1], (D,), jnp.float32), 0.5, 1.5),
        "w_query": draw_w_query(jax.random.fold_in(key_of[13], 71), 0),
        "w_key": draw_w_key(jax.random.fold_in(key_of[13], 71), 0),
        "w_value": normal_values(key_of[4], (D, KV_HEADS * HEAD_DIM), D ** -0.5, 0.078125, ((0, 32), (1, 4))),
        "w_out": normal_values(key_of[5], (HEADS * HEAD_DIM, D), (HEADS * HEAD_DIM) ** -0.5, 0.125, ((0, 4), (1, 32))),
        "q_gain": draw_q_gain(jax.random.fold_in(key_of[13], 71), 0),
        "k_gain": draw_k_gain(jax.random.fold_in(key_of[13], 71), 0),
        "post_gain": jnp.clip(1.0 + 0.1 * jax.random.normal(key_of[8], (D,), jnp.float32), 0.5, 1.5),
        "final_gain": draw_final_gain(jax.random.fold_in(key_of[13], 71), 0),
        "lm_head": draw_lm_head(jax.random.fold_in(key_of[13], 71), 0),
        "targets": touch_ends(jax.random.randint(key_of[11], (TOKENS,), 0, VOCAB), jax.random.fold_in(key_of[11], 1), 0, VOCAB - 1).astype(jnp.int32),
        "positions": draw_positions(jax.random.fold_in(key_of[13], 71), 0),
    }


epsilon = 1e-06
query_scale = 168.0 ** (-0.5)

def rms_norm(values, gain):
    mean_sq = lax.optimization_barrier(jnp.mean(values * values, axis=-1, keepdims=True))
    return values * lax.rsqrt(mean_sq + epsilon) * gain

def rotate_pos(values, places):
    half_dim = values.shape[-1] // 2
    exponent = jnp.arange(half_dim, dtype=jnp.float32) * (2.0 / values.shape[-1])
    freqs = jnp.exp(-exponent * jnp.log(jnp.float32(1000000.0)))
    angles = (places / 8.0)[:, None] * freqs[None, :]
    cosine = jnp.cos(angles)[:, None, :]
    sine = jnp.sin(angles)[:, None, :]
    first_half = values[..., :half_dim]
    second_half = values[..., half_dim:]
    return jnp.concatenate([first_half * cosine - second_half * sine, second_half * cosine + first_half * sine], axis=-1)

def reference(hidden, attn_gain, w_query, w_key, w_value, w_out, q_gain, k_gain, post_gain, final_gain, lm_head, targets, positions):
    residual = hidden.astype(jnp.float32)
    normed = rms_norm(residual, attn_gain).astype(jnp.bfloat16)
    queries = jnp.dot(normed, w_query, preferred_element_type=jnp.float32).reshape(TOKENS, HEADS, HEAD_DIM)
    keys_raw = jnp.dot(normed, w_key, preferred_element_type=jnp.float32).reshape(TOKENS, KV_HEADS, HEAD_DIM)
    v_low = jnp.dot(normed, w_value, preferred_element_type=jnp.float32).astype(jnp.bfloat16).reshape(TOKENS, KV_HEADS, HEAD_DIM)
    places = positions.astype(jnp.float32)
    q_rot = (rotate_pos(rms_norm(queries, q_gain), places) * query_scale).astype(jnp.bfloat16)
    k_rot = rotate_pos(rms_norm(keys_raw, k_gain), places).astype(jnp.bfloat16)
    q_rot, k_rot, v_low = lax.optimization_barrier((q_rot, k_rot, v_low))
    token_index = jnp.arange(TOKENS, dtype=jnp.int32)
    doc_base = positions.astype(jnp.int32) - token_index
    block = math.gcd(TOKENS, 512)
    q_group = q_rot.reshape(TOKENS, KV_HEADS, HEADS // KV_HEADS, HEAD_DIM)
    keys_wide = k_rot.astype(jnp.float32)
    values_wide = v_low.astype(jnp.float32)

    def one_block(begin):
        q_part = lax.dynamic_slice_in_dim(q_group, begin, block, 0).astype(jnp.float32)
        rows_index = lax.dynamic_slice_in_dim(token_index, begin, block, 0)
        doc_part = lax.dynamic_slice_in_dim(doc_base, begin, block, 0)
        scores = jnp.einsum('bkgd,skd->kgbs', q_part, keys_wide)
        visible = (token_index[None, :] <= rows_index[:, None]) & (doc_base[None, :] == doc_part[:, None])
        masked = jnp.where(visible, scores, -1e+30)
        top_score = lax.optimization_barrier(jnp.max(masked, axis=-1, keepdims=True))
        expo = jnp.where(visible, jnp.exp(masked - top_score), 0.0)
        probs = lax.optimization_barrier(expo.astype(jnp.bfloat16)).astype(jnp.float32)
        mixed = jnp.einsum('kgbs,skd->kgbd', probs, values_wide) / lax.optimization_barrier(jnp.sum(expo, axis=-1))[..., None]
        return jnp.transpose(mixed, (2, 0, 1, 3)).reshape(block, HEADS * HEAD_DIM).astype(jnp.bfloat16)
    starts = jnp.arange(TOKENS // block, dtype=jnp.int32) * block
    attended = lax.map(one_block, starts).reshape(TOKENS, HEADS * HEAD_DIM)
    projected = jnp.dot(attended, w_out, preferred_element_type=jnp.float32)
    layer_full = (residual + rms_norm(projected, post_gain)).astype(jnp.bfloat16)
    final_rows = rms_norm(layer_full.astype(jnp.float32), final_gain).astype(jnp.bfloat16)
    logits = jnp.dot(final_rows, lm_head.T, preferred_element_type=jnp.float32)
    top_logit = lax.optimization_barrier(jnp.max(logits, axis=1))
    log_total = jnp.log(lax.optimization_barrier(jnp.sum(jnp.exp(logits - top_logit[:, None]), axis=1)))
    target_logit = jnp.take_along_axis(logits, targets.astype(jnp.int32)[:, None], axis=1)[:, 0]
    return (target_logit - top_logit - log_total, layer_full)
```

```python
import functools
import math

import jax
import jax.numpy as jnp
from jax import lax
from jax.experimental import pallas as pl
from jax.experimental.pallas import tpu as pltpu
from jax.sharding import PartitionSpec as P

BF16 = jnp.bfloat16
F32 = jnp.float32
I32 = jnp.int32
EPS = 1e-06
QUERY_SCALE = 168.0 ** (-0.5) * math.log2(math.e)
LOW = -1e30
MIB = 1024 * 1024

PLANS = (("z", 1, "x", 1), ("z", -1, "x", -1), ("x", 1, "z", 1), ("x", -1, "z", -1))


def place_of(device):
    ctx, tp = divmod(device, 4)
    return {"z": ctx // 8, "x": (ctx // 2) % 4, "y": (tp // 2) * 2 + ctx % 2, "core": tp % 2}


def device_of(place):
    y = place["y"] % 4
    ctx = (place["z"] % 4) * 8 + (place["x"] % 4) * 2 + y % 2
    return ctx * 4 + (y // 2) * 2 + place["core"] % 2


def send(value, move):
    pairs = []
    for device in range(128):
        place = place_of(device)
        pairs.append((device, device_of({**place, **move(place)})))
    return lax.ppermute(value, ("ctx", "tp"), pairs)


def shift(value, axis, step):
    return send(value, lambda place: {axis: place[axis] + step})


def other_core(value):
    return shift(value, "core", 1)


def other_half(value):
    return send(value, lambda place: {"y": place["y"] ^ 1})


def plane_gather(parts, axis):
    rows = [[part] for part in parts]
    for _ in range(3):
        for row, plan in zip(rows, PLANS):
            row.append(shift(row[-1], plan[0], plan[1]))
    planes = [[jnp.stack(row, axis=axis)] for row in rows]
    for _ in range(3):
        for plane, plan in zip(planes, PLANS):
            plane.append(shift(plane[-1], plan[2], plan[3]))
    return planes


def back(me, distance, direction):
    return (me - distance * direction + 8) & 3


def source(me, plan, far, near):
    at = {plan[0]: back(me[plan[0]], near, plan[1]), plan[2]: back(me[plan[2]], far, plan[3])}
    return at["z"], at["x"]


def read_me(me_ref):
    return {"z": me_ref[0], "x": me_ref[1], "y": me_ref[2], "core": me_ref[3]}


def normalize(value, gain):
    mean_sq = jnp.mean(value * value, axis=-1, keepdims=True)
    return value * lax.rsqrt(mean_sq + EPS) * gain


def qkv_kernel(me_ref, *refs):
    hidden_refs = refs[:8]
    weight_refs = [refs[8 + 4 * p : 12 + 4 * p] for p in range(4)]
    gain_ref, q_gain_ref, k_gain_ref, cos_ref, sin_ref, q_ref, kv_ref = refs[24:31]
    weights, blocks, total, squares, weight_sem, block_sem = refs[31:]
    me = read_me(me_ref)
    depth = blocks.shape[2]
    copies = []
    for i in range(8):
        pltpu.make_async_copy(hidden_refs[i], blocks.at[i], block_sem.at[i]).start()
    for p in range(4):
        rows = weight_refs[p][0].shape[1]
        for far in range(4):
            for near in range(4):
                z, x = source(me, PLANS[p], far, near)
                start = pl.multiple_of((z * 4 + x) * rows, 16)
                copy = pltpu.make_async_copy(
                    weight_refs[p][far].at[near],
                    weights.at[pl.ds(start, rows), pl.ds(128 * p, 128)],
                    weight_sem.at[p * 16 + far * 4 + near],
                )
                copy.start()
                copies.append(copy)
    total[...] = jnp.zeros_like(total)
    squares[...] = jnp.zeros_like(squares)
    for copy in copies:
        copy.wait()
    turn = 1 - 2 * me["core"]

    @pl.loop(0, 8)
    def _(i):
        pltpu.make_async_copy(hidden_refs[0], blocks.at[i], block_sem.at[i]).wait()
        swapped = i // 4
        y = (me["y"] - (i & 3) * turn * (1 - 2 * swapped) + 8) & 3
        half = y & 1
        group = (y // 2) * 2 + (me["core"] ^ swapped)
        block = blocks[i].astype(F32)
        squares[half] += jnp.broadcast_to(jnp.sum(block * block, axis=1, keepdims=True), squares.shape[1:])
        scaled = (block * gain_ref[group]).astype(BF16)
        start = pl.multiple_of(group * depth, 64)
        total[half] += jnp.dot(scaled, weights[pl.ds(start, depth), :], preferred_element_type=F32)

    rows = total.shape[1]
    for half in range(2):
        scale = lax.rsqrt(squares[half] * (1.0 / (4 * depth)) + EPS)
        cosine = cos_ref[pl.ds(half * rows, rows), :]
        sine = sin_ref[pl.ds(half * rows, rows), :]

        def rotate(value):
            return value * cosine + pltpu.roll(value, 64, 1) * sine

        for head in range(2):
            query = normalize(total[half, :, pl.ds(128 * head, 128)] * scale, q_gain_ref[...])
            q_ref[head, pl.ds(half * rows, rows), :] = (rotate(query) * QUERY_SCALE).astype(BF16)
        key = rotate(normalize(total[half, :, pl.ds(256, 128)] * scale, k_gain_ref[...])).astype(BF16)
        value = (total[half, :, pl.ds(384, 128)] * scale).astype(BF16)
        for quarter in range(2):
            cut = slice(quarter * rows // 2, (quarter + 1) * rows // 2)
            kv_ref[2 * half + quarter, 0] = key[cut]
            kv_ref[2 * half + quarter, 1] = value[cut]


def attend_kernel(first, last, far, me_ref, low_ref, q_ref, kv0, kv1, kv2, kv3, low_col, *refs):
    kvs = (kv0, kv1, kv2, kv3)
    if first:
        refs = (None, None) + refs
    top_in, total_in, *refs = refs
    if last:
        out_ref, top, total, wide = refs
    else:
        top, total, wide = refs
    if first:
        top[...] = jnp.full_like(top, LOW)
        total[...] = jnp.zeros_like(total)
    else:
        top[...] = top_in[...]
        total[...] = total_in[...]
    me = read_me(me_ref)
    quarter = kv0.shape[2]
    tokens = 4 * quarter
    tile = 256
    per_head = tokens // tile
    begin = (me["z"] * 4 + me["x"]) * tokens
    wide[:, 128:] = jnp.ones((tokens, 128), BF16)
    for p in range(4):
        wide[:, :128] = kvs[p][1].reshape(tokens, 128)
        bases = []
        for near in range(4):
            z, x = source(me, PLANS[p], far, near)
            bases.append((z * 4 + x) * tokens + p * quarter)

        @pl.loop(0, 2 * per_head)
        def _(step):
            piece = lax.rem(step, per_head)
            row = pl.multiple_of(step * tile, tile)
            token = pl.multiple_of(piece * tile, tile)
            q_first = begin + token
            q_last = q_first + tile - 1
            low_first = low_ref[2 * piece]
            low_last = low_ref[2 * piece + 1]
            seen = [(b <= q_last) & (b + quarter - 1 >= low_first) for b in bases]
            whole = [(b + quarter - 1 <= q_first) & (b >= low_last) for b in bases]
            some = functools.reduce(jnp.logical_or, seen)
            every = functools.reduce(jnp.logical_and, whole)

            def work(masked):
                keys = kvs[p][0].reshape(tokens, 128)
                scores = lax.dot_general(
                    q_ref[pl.ds(row, tile), :], keys, (((1,), (1,)), ((), ())), preferred_element_type=F32
                )
                if masked:
                    lane = lax.broadcasted_iota(I32, (1, tokens), 1)
                    index = bases[0] + lane
                    for near in range(1, 4):
                        index = jnp.where(lane >= near * quarter, bases[near] - near * quarter + lane, index)
                    own = q_first + lax.broadcasted_iota(I32, (tile, 1), 0)
                    visible = (index <= own) & (index >= low_col[pl.ds(token, tile), :])
                    scores = jnp.where(visible, scores, LOW)
                before = top[pl.ds(row, tile), :]
                now = jnp.maximum(before, jnp.max(scores, axis=1, keepdims=True))
                probs = jnp.exp2(scores - jnp.concatenate([now] * (tokens // 128), axis=1)).astype(BF16)
                fade = jnp.exp2(before - now)
                top[pl.ds(row, tile), :] = now
                total[pl.ds(row, tile), :] = total[pl.ds(row, tile), :] * jnp.concatenate(
                    [fade, fade], axis=1
                ) + jnp.dot(probs, wide[...], preferred_element_type=F32)

            @pl.when(some & every)
            def _():
                work(False)

            @pl.when(some & jnp.logical_not(every))
            def _():
                work(True)

    if last:
        for head in range(2):
            rows = pl.ds(head * tokens, tokens)
            out_ref[:, pl.ds(head * 128, 128)] = (total[rows, pl.ds(0, 128)] / total[rows, pl.ds(128, 128)]).astype(BF16)


def spread_kernel(me_ref, *refs):
    parts = [refs[4 * p : 4 * p + 4] for p in range(4)]
    outs = refs[16:24]
    sem = refs[24]
    me = read_me(me_ref)
    waits = []
    for dy in range(4):
        for dc in range(2):
            out = outs[2 * dy + dc]
            z = (me["y"] + dy) & 3
            core = me["core"] ^ dc
            for side in range(2):
                at = {"z": z, "x": 2 * core + side}
                row = 0
                for p in range(4):
                    plan = PLANS[p]
                    rows = parts[p][0].shape[1]
                    row = 0 if p < 2 else parts[0][0].shape[1]
                    far = ((me[plan[2]] - at[plan[2]]) * plan[3] + 8) & 3
                    near = ((me[plan[0]] - at[plan[0]]) * plan[1] + 8) & 3
                    target = out.at[side, pl.ds(row, rows), pl.ds(128 * (p % 2), 128)]
                    flag = sem.at[(2 * dy + dc) * 8 + side * 4 + p]
                    for j in range(4):

                        @pl.when(far == j)
                        def _():
                            pltpu.make_async_copy(parts[p][j].at[near], target, flag).start()

                    waits.append(pltpu.make_async_copy(parts[p][0].at[0], target, flag))
    for wait in waits:
        wait.wait()


def project_kernel(me_ref, *refs):
    attended = refs[:8]
    weights = refs[8:16]
    outs = refs[16:18]
    half = me_ref[2] & 1
    rows = outs[0].shape[0]
    for side in range(2):
        start = pl.multiple_of((half ^ side) * rows, 128)
        total = None
        for a, w in zip(attended, weights):
            term = lax.dot_general(
                a[pl.ds(start, rows), :], w[...], (((1,), (1,)), ((), ())), preferred_element_type=F32
            )
            total = term if total is None else total + term
        outs[side][...] = total.astype(BF16)


def logits_kernel(me_ref, *refs):
    hidden_refs = refs[:4]
    piece_refs = refs[4:12]
    post_ref, final_ref, targets_ref, head_ref, layer_ref, stats_ref = refs[12:18]
    residual, pieces, layers, rows_all, top, total, picked, hidden_sem, piece_sem = refs[18:]
    me = read_me(me_ref)
    step = pl.program_id(0)
    tp = (me["y"] // 2) * 2 + me["core"]
    width = layer_ref.shape[1]
    tokens = layer_ref.shape[0]
    count = width * 4

    @pl.when(step == 0)
    def _():
        copies = []
        for i, ref in enumerate(hidden_refs):
            group = tp ^ ((0, 2, 1, 3)[i])
            copies.append(pltpu.make_async_copy(ref, residual.at[group], hidden_sem.at[i]))
        for dy in range(4):
            for dc in range(2):
                copies.append(
                    pltpu.make_async_copy(
                        piece_refs[2 * dy + dc],
                        pieces.at[(me["y"] - dy + 4) & 3, me["core"] ^ dc],
                        piece_sem.at[2 * dy + dc],
                    )
                )
        for copy in copies:
            copy.start()
        top[...] = jnp.full_like(top, -jnp.inf)
        total[...] = jnp.zeros_like(total)
        picked[...] = jnp.zeros_like(picked)
        for copy in copies:
            copy.wait()

        square = jnp.zeros((tokens, 1), F32)
        for y in range(4):
            for core in range(2):
                piece = pieces[y, core].astype(F32)
                square += jnp.sum(piece * piece, axis=1, keepdims=True)
        scale = lax.rsqrt(square * (1.0 / count) + EPS)
        square = jnp.zeros((tokens, 1), F32)
        for y in range(4):
            joined = jnp.concatenate([pieces[y, 0].astype(F32), pieces[y, 1].astype(F32)], axis=1)
            layer = (residual[y].astype(F32) + joined * scale * post_ref[y]).astype(BF16)
            layers[y] = layer
            wide = layer.astype(F32)
            square += jnp.sum(wide * wide, axis=1, keepdims=True)
        layer_ref[...] = layers[tp]
        scale = lax.rsqrt(square * (1.0 / count) + EPS)
        for y in range(4):
            rows_all[:, pl.ds(y * width, width)] = (layers[y].astype(F32) * scale * final_ref[y]).astype(BF16)

    logits = lax.dot_general(rows_all[...], head_ref[...], (((1,), (1,)), ((), ())), preferred_element_type=F32)
    before = top[...]
    now = jnp.maximum(before, jnp.max(logits, axis=1, keepdims=True))
    top[...] = now
    total[...] = total[...] * jnp.exp(before - now) + jnp.sum(
        jnp.exp(logits - now[:, :1]), axis=1, keepdims=True
    )
    block = head_ref.shape[0]
    first = (tp * pl.num_programs(0) + step) * block
    index = first + lax.broadcasted_iota(I32, (1, block), 1)
    picked[...] += jnp.sum(jnp.where(index == targets_ref[...], logits, 0.0), axis=1, keepdims=True)

    @pl.when(step == pl.num_programs(0) - 1)
    def _():
        lane = lax.broadcasted_iota(I32, top.shape, 1)
        stats_ref[...] = jnp.where(lane == 0, top[...], jnp.where(lane == 1, total[...], picked[...]))


def params(mib, **extra):
    return pltpu.CompilerParams(vmem_limit_bytes=mib * MIB, **extra)


SMEM = pl.BlockSpec(memory_space=pltpu.SMEM)
VMEM = pl.BlockSpec(memory_space=pltpu.VMEM)
ANY = pl.BlockSpec(memory_space=pl.ANY)


def on_device(
    hidden, attn_gain, w_query, w_key, w_value, w_out, q_gain, k_gain, post_gain, final_gain, lm_head, targets, positions
):
    rows, width = hidden.shape
    tokens = 2 * rows
    quarter = rows // 2
    ctx_rank = lax.axis_index("ctx")
    tp_rank = lax.axis_index("tp")
    half = ctx_rank % 2
    z, x, y, core = ctx_rank // 8, (ctx_rank // 2) % 4, (tp_rank // 2) * 2 + half, tp_rank % 2
    me = jnp.stack([z, x, y, core]).astype(I32)

    def both_halves(own, received, axis):
        return jnp.where(
            half == 0, jnp.concatenate([own, received], axis), jnp.concatenate([received, own], axis)
        )

    def columns_of(side):
        return jnp.concatenate(
            [
                lax.dynamic_slice_in_dim(w_query, side * 256, 256, 1),
                lax.dynamic_slice_in_dim(w_key, side * 128, 128, 1),
                lax.dynamic_slice_in_dim(w_value, side * 128, 128, 1),
            ],
            axis=1,
        )

    other_weights = other_half(columns_of(1 - half))
    other_positions = other_half(positions)
    weights = both_halves(columns_of(half), other_weights, 0)

    ring = [hidden]
    for _ in range(3):
        ring.append(send(ring[-1], lambda place: {"y": place["y"] + 1 - 2 * place["core"]}))
    swapped = [other_core(block) for block in ring]
    gathered = plane_gather([weights[:, 128 * p : 128 * p + 128] for p in range(4)], 0)

    places = both_halves(positions, other_positions, 0)
    token = (z * 4 + x) * tokens + jnp.arange(tokens, dtype=I32)
    low = jnp.maximum(token - places, 0)
    exponent = jnp.arange(64, dtype=F32) * (2.0 / 128)
    freqs = jnp.exp(-exponent * jnp.log(F32(1000000.0)))
    angles = (places.astype(F32) / 8.0)[:, None] * freqs[None, :]
    cosine, sine = jnp.cos(angles), jnp.sin(angles)
    cosine = jnp.concatenate([cosine, cosine], axis=1)
    sine = jnp.concatenate([-sine, sine], axis=1)

    queries, kv = pl.pallas_call(
        qkv_kernel,
        out_shape=(
            jax.ShapeDtypeStruct((2, tokens, 128), BF16),
            jax.ShapeDtypeStruct((4, 2, quarter, 128), BF16),
        ),
        in_specs=[SMEM] + [ANY] * 24 + [VMEM] * 5,
        out_specs=(VMEM, VMEM),
        scratch_shapes=[
            pltpu.VMEM((4 * width, 512), BF16),
            pltpu.VMEM((8, rows, width), BF16),
            pltpu.VMEM((2, rows, 512), F32),
            pltpu.VMEM((2, rows, 128), F32),
            pltpu.SemaphoreType.DMA((64,)),
            pltpu.SemaphoreType.DMA((8,)),
        ],
        compiler_params=params(40),
        cost_estimate=pl.CostEstimate(flops=4300000000, bytes_accessed=14000000, transcendentals=0),
        name="qkv",
    )(
        me,
        *ring,
        *swapped,
        *[block for plane in gathered for block in plane],
        attn_gain.reshape(4, 1, width),
        q_gain.reshape(1, 128),
        k_gain.reshape(1, 128),
        cosine,
        sine,
    )
    queries = queries.reshape(2 * tokens, 128)

    chunks = plane_gather([kv[p] for p in range(4)], 1)
    edges = low.reshape(-1, 256)
    edges = jnp.stack([edges[:, 0], edges[:, -1]], axis=1).reshape(-1)
    low_col = low.reshape(tokens, 1)
    state = ()
    state_shape = (
        jax.ShapeDtypeStruct((2 * tokens, 128), F32),
        jax.ShapeDtypeStruct((2 * tokens, 256), F32),
    )
    for far in range(4):
        first, last = far == 0, far == 3
        call = pl.pallas_call(
            functools.partial(attend_kernel, first, last, far),
            out_shape=jax.ShapeDtypeStruct((tokens, 256), BF16) if last else state_shape,
            in_specs=[SMEM, SMEM] + [VMEM] * (6 + len(state)),
            out_specs=VMEM if last else (VMEM, VMEM),
            scratch_shapes=(
                [pltpu.VMEM((2 * tokens, 128), F32), pltpu.VMEM((2 * tokens, 256), F32)] if last else []
            )
            + [pltpu.VMEM((tokens, 256), BF16)],
            compiler_params=params(32),
            cost_estimate=pl.CostEstimate(flops=4800000000, bytes_accessed=8000000, transcendentals=4700000),
            name=f"attend{far}",
        )
        state = call(me, edges, queries, *[chunks[p][far] for p in range(4)], low_col, *state)
    attended = state

    other_out = other_half(lax.dynamic_slice_in_dim(w_out, (1 - half) * 256, 256, 0).T)
    out_rows = both_halves(lax.dynamic_slice_in_dim(w_out, half * 256, 256, 0).T, other_out, 0)
    feats = out_rows.shape[0]
    cut = (feats // 2 + 15) // 16 * 16
    out_parts = plane_gather(
        [out_rows[:cut, :128], out_rows[:cut, 128:], out_rows[cut:, :128], out_rows[cut:, 128:]], 0
    )
    spread = pl.pallas_call(
        spread_kernel,
        out_shape=[jax.ShapeDtypeStruct((2, feats, 256), BF16)] * 8,
        in_specs=[SMEM] + [ANY] * 16,
        out_specs=[ANY] * 8,
        scratch_shapes=[pltpu.SemaphoreType.DMA((64,))],
        compiler_params=params(8),
        cost_estimate=pl.CostEstimate(flops=0, bytes_accessed=6000000, transcendentals=0),
        name="spread",
    )(me, *[block for plane in out_parts for block in plane])
    own_out = []
    for dy in range(4):
        for dc in range(2):
            block = spread[2 * dy + dc]
            if dy or dc:
                block = send(
                    block, lambda place, dy=dy, dc=dc: {"y": place["y"] + dy, "core": place["core"] + dc}
                )
            own_out.append(block.reshape(2 * feats, 256))

    column = []
    for dy in range(4):
        block = shift(attended, "y", dy) if dy else attended
        column += [block, other_core(block)]
    same, across = pl.pallas_call(
        project_kernel,
        out_shape=[jax.ShapeDtypeStruct((rows, 2 * feats), BF16)] * 2,
        in_specs=[SMEM] + [VMEM] * 16,
        out_specs=[VMEM] * 2,
        compiler_params=params(32),
        cost_estimate=pl.CostEstimate(flops=2100000000, bytes_accessed=7000000, transcendentals=0),
        name="project",
    )(me, *column, *own_out)

    pieces = []
    for dy in range(4):
        block = same if dy == 0 else shift(across if dy % 2 else same, "y", dy)
        pieces += [block, other_core(block)]

    block = 256
    steps = lm_head.shape[0] // block
    whole2 = lambda i: (0, 0)
    whole3 = lambda i: (0, 0, 0)
    layer_out, stats = pl.pallas_call(
        logits_kernel,
        grid=(steps,),
        out_shape=(jax.ShapeDtypeStruct((rows, width), BF16), jax.ShapeDtypeStruct((rows, 128), F32)),
        in_specs=[SMEM]
        + [ANY] * 12
        + [
            pl.BlockSpec((4, 1, width), whole3),
            pl.BlockSpec((4, 1, width), whole3),
            pl.BlockSpec((rows, 1), whole2),
            pl.BlockSpec((block, 4 * width), lambda i: (i, 0)),
        ],
        out_specs=(pl.BlockSpec((rows, width), whole2), pl.BlockSpec((rows, 128), whole2)),
        scratch_shapes=[
            pltpu.VMEM((4, rows, width), BF16),
            pltpu.VMEM((4, 2, rows, width // 2), BF16),
            pltpu.VMEM((4, rows, width), BF16),
            pltpu.VMEM((rows, 4 * width), BF16),
            pltpu.VMEM((rows, 128), F32),
            pltpu.VMEM((rows, 128), F32),
            pltpu.VMEM((rows, 128), F32),
            pltpu.SemaphoreType.DMA((4,)),
            pltpu.SemaphoreType.DMA((8,)),
        ],
        compiler_params=params(48),
        cost_estimate=pl.CostEstimate(flops=8500000000, bytes_accessed=32000000, transcendentals=800000),
        name="logits",
    )(
        me,
        ring[0],
        ring[2],
        swapped[0],
        swapped[2],
        *pieces,
        post_gain.reshape(4, 1, width),
        final_gain.reshape(4, 1, width),
        targets.reshape(rows, 1),
        lm_head,
    )
    shared = lax.all_gather(stats[:, :3], "tp")
    largest = jnp.max(shared[:, :, 0], axis=0)
    total = jnp.sum(shared[:, :, 1] * jnp.exp(shared[:, :, 0] - largest), axis=0)
    target_logit = jnp.sum(shared[:, :, 2], axis=0)
    logprobs = target_logit - largest - jnp.log(total)
    return (logprobs, layer_out)


def solution(mesh):
    return jax.shard_map(
        on_device,
        mesh=mesh,
        in_specs=(
            P("ctx", "tp"),
            P(),
            P("ctx", "tp"),
            P("ctx", "tp"),
            P("ctx", "tp"),
            P("tp", "ctx"),
            P(),
            P(),
            P(),
            P(),
            P("tp", None),
            P("ctx"),
            P("ctx"),
        ),
        out_specs=(P("ctx"), P("ctx", "tp")),
        check_vma=False,
    )
```

```python
import functools
import math

import jax
import jax.numpy as jnp
from jax import lax
from jax.experimental import pallas as pl
from jax.experimental.pallas import tpu as pltpu
from jax.sharding import Mesh
from jax.sharding import PartitionSpec as P

BF16 = jnp.bfloat16
F32 = jnp.float32
I32 = jnp.int32
EPS = 1e-06
QUERY_SCALE = 168.0 ** (-0.5) * math.log2(math.e)
LOW = -1e30
MIB = 1024 * 1024

PLANS = (("z", "x"), ("x", "z"))
AXES = ("z", "x", "yl", "yh", "core")
SIZES = (4, 4, 2, 2, 2)


def place_of(device):
    place = {}
    for axis, size in zip(reversed(AXES), reversed(SIZES)):
        device, place[axis] = divmod(device, size)
    place["y"] = 2 * place["yh"] + place["yl"]
    return place


def device_of(place):
    y = place["y"] % 4
    place = {**place, "yh": y // 2, "yl": y % 2}
    device = 0
    for axis, size in zip(AXES, SIZES):
        device = device * size + place[axis] % size
    return device


def send(value, move):
    pairs = []
    for device in range(128):
        place = place_of(device)
        pairs.append((device, device_of({**place, **move(place)})))
    return lax.ppermute(value, AXES, pairs)


def shift(value, axis, step):
    return send(value, lambda place: {axis: place[axis] + step})


def turn(value, axis):
    return send(value, lambda place: {axis: place[axis] + 1 - 2 * place["core"]})


def other_core(value):
    return shift(value, "core", 1)


def other_half(value):
    return send(value, lambda place: {"y": place["y"] ^ 1})


def plane_gather(parts, axis):
    rows = [[part] for part in parts]
    for _ in range(3):
        for row, plan in zip(rows, PLANS):
            row.append(turn(row[-1], plan[0]))
    planes = [[jnp.stack(row, axis=axis)] for row in rows]
    for _ in range(3):
        for plane, plan in zip(planes, PLANS):
            plane.append(turn(plane[-1], plan[1]))
    return planes


def back(me, axis, distance):
    return (me[axis] - distance * (1 - 2 * me["core"]) + 8) & 3


def source(me, plan, far, near):
    at = {plan[0]: back(me, plan[0], near), plan[1]: back(me, plan[1], far)}
    return at["z"], at["x"]


def read_me(me_ref):
    return {"z": me_ref[0], "x": me_ref[1], "y": me_ref[2], "core": me_ref[3]}


def normalize(value, gain):
    mean_sq = jnp.mean(value * value, axis=-1, keepdims=True)
    return value * lax.rsqrt(mean_sq + EPS) * gain


def block_place(me, i):
    swapped = i // 4
    y = (me["y"] - (i & 3) * (1 - 2 * me["core"]) * (1 - 2 * swapped) + 8) & 3
    return y & 1, (y // 2) * 2 + (me["core"] ^ swapped)


def rotate(value, cosine, sine):
    return value * cosine + pltpu.roll(value, 64, 1) * sine


def keys_kernel(me_ref, *refs):
    blocks = refs[:8]
    weight_ref, gain_ref, k_gain_ref, cos_ref, sin_ref, kv_ref, squares = refs[8:15]
    weights, total, sem = refs[15:]
    me = read_me(me_ref)
    rows, depth = blocks[0].shape
    copy = pltpu.make_async_copy(weight_ref, weights, sem)
    copy.start()
    total[...] = jnp.zeros_like(total)
    squares[...] = jnp.zeros_like(squares)
    copy.wait()
    for i in range(8):
        half, group = block_place(me, i)
        block = blocks[i][...].astype(F32)
        squares[half] += jnp.broadcast_to(jnp.sum(block * block, axis=1, keepdims=True), squares.shape[1:])
        scaled = (block * gain_ref[group]).astype(BF16)
        start = pl.multiple_of(group * depth, 64)
        total[half] += jnp.dot(scaled, weights[pl.ds(start, depth), :], preferred_element_type=F32)
    for half in range(2):
        scale = lax.rsqrt(squares[half] * (1.0 / (4 * depth)) + EPS)
        cut = pl.ds(half * rows, rows)
        key = normalize(total[half, :, pl.ds(0, 128)] * scale, k_gain_ref[...])
        kv_ref[half, 0] = rotate(key, cos_ref[cut, :], sin_ref[cut, :]).astype(BF16)
        kv_ref[half, 1] = (total[half, :, pl.ds(128, 128)] * scale).astype(BF16)


def queries_kernel(me_ref, *refs):
    blocks = refs[:8]
    parts = [refs[8:12], refs[12:16]]
    gain_ref, q_gain_ref, cos_ref, sin_ref, squares, q_ref = refs[16:22]
    weights, total, sem = refs[22:]
    me = read_me(me_ref)
    rows, depth = blocks[0].shape
    copies = []
    for p in range(2):
        height = parts[p][0].shape[1]
        for far in range(4):
            for near in range(4):
                z, x = source(me, PLANS[p], far, near)
                start = pl.multiple_of((z * 4 + x) * height, 16)
                copies.append(
                    pltpu.make_async_copy(
                        parts[p][far].at[near],
                        weights.at[pl.ds(start, height), pl.ds(128 * p, 128)],
                        sem.at[p * 16 + far * 4 + near],
                    )
                )
    for copy in copies:
        copy.start()
    total[...] = jnp.zeros_like(total)
    for copy in copies:
        copy.wait()
    for i in range(8):
        half, group = block_place(me, i)
        scaled = (blocks[i][...].astype(F32) * gain_ref[group]).astype(BF16)
        start = pl.multiple_of(group * depth, 64)
        total[half] += jnp.dot(scaled, weights[pl.ds(start, depth), :], preferred_element_type=F32)
    for half in range(2):
        scale = lax.rsqrt(squares[half] * (1.0 / (4 * depth)) + EPS)
        cut = pl.ds(half * rows, rows)
        for head in range(2):
            query = normalize(total[half, :, pl.ds(128 * head, 128)] * scale, q_gain_ref[...])
            q_ref[head, cut, :] = (rotate(query, cos_ref[cut, :], sin_ref[cut, :]) * QUERY_SCALE).astype(BF16)


def attend_kernel(first, last, far, me_ref, low_ref, q_ref, low_col, *refs):
    count = 1 if far is None else 2
    kvs, refs = refs[:count], refs[count:]
    if first:
        refs = (None, None) + refs
    top_in, total_in, *refs = refs
    if last:
        out_ref, top, total, wide = refs
    else:
        top, total, wide = refs
    if first:
        top[...] = jnp.full_like(top, LOW)
        total[...] = jnp.zeros_like(total)
    else:
        top[...] = top_in[...]
        total[...] = total_in[...]
    me = read_me(me_ref)
    tokens = q_ref.shape[0] // 2
    tile = 256
    per_head = tokens // tile
    begin = (me["z"] * 4 + me["x"]) * tokens
    wide[:, 128:] = jnp.ones((tokens, 128), BF16)

    def attend(keys, values, bases, length):
        wide[:, :128] = values

        @pl.loop(0, 2 * per_head)
        def _(step):
            piece = lax.rem(step, per_head)
            row = pl.multiple_of(step * tile, tile)
            token = pl.multiple_of(piece * tile, tile)
            q_first = begin + token
            q_last = q_first + tile - 1
            low_first = low_ref[2 * piece]
            low_last = low_ref[2 * piece + 1]
            seen = [(b <= q_last) & (b + length - 1 >= low_first) for b in bases]
            whole = [(b + length - 1 <= q_first) & (b >= low_last) for b in bases]
            some = functools.reduce(jnp.logical_or, seen)
            every = functools.reduce(jnp.logical_and, whole)

            def work(masked):
                scores = lax.dot_general(
                    q_ref[pl.ds(row, tile), :], keys(), (((1,), (1,)), ((), ())), preferred_element_type=F32
                )
                if masked:
                    lane = lax.broadcasted_iota(I32, (1, tokens), 1)
                    index = bases[0] + lane
                    for near in range(1, len(bases)):
                        index = jnp.where(lane >= near * length, bases[near] - near * length + lane, index)
                    own = q_first + lax.broadcasted_iota(I32, (tile, 1), 0)
                    visible = (index <= own) & (index >= low_col[pl.ds(token, tile), :])
                    scores = jnp.where(visible, scores, LOW)
                before = top[pl.ds(row, tile), :]
                now = jnp.maximum(before, jnp.max(scores, axis=1, keepdims=True))
                probs = jnp.exp2(scores - jnp.concatenate([now] * (tokens // 128), axis=1)).astype(BF16)
                fade = jnp.exp2(before - now)
                top[pl.ds(row, tile), :] = now
                total[pl.ds(row, tile), :] = total[pl.ds(row, tile), :] * jnp.concatenate(
                    [fade, fade], axis=1
                ) + jnp.dot(probs, wide[...], preferred_element_type=F32)

            @pl.when(some & every)
            def _():
                work(False)

            @pl.when(some & jnp.logical_not(every))
            def _():
                work(True)

    if far is None:
        length = kvs[0].shape[2]

        @pl.loop(0, kvs[0].shape[0] // 2)
        def _(pair):
            pick = lambda which: jnp.concatenate([kvs[0][2 * pair, which], kvs[0][2 * pair + 1, which]], axis=0)
            bases = [(2 * pair + i) * tokens for i in range(2)]
            attend(lambda: pick(0), pick(1), bases, length)

    else:
        for p in range(2):
            length = kvs[p].shape[2]
            bases = []
            for near in range(4):
                z, x = source(me, PLANS[p], far, near)
                bases.append((z * 4 + x) * tokens + (2 + p) * length)
            attend(lambda: kvs[p][0].reshape(tokens, 128), kvs[p][1].reshape(tokens, 128), bases, length)

    if last:
        for head in range(2):
            rows = pl.ds(head * tokens, tokens)
            out_ref[:, pl.ds(head * 128, 128)] = (total[rows, pl.ds(0, 128)] / total[rows, pl.ds(128, 128)]).astype(BF16)


def project_kernel(me_ref, *refs):
    attended = refs[:8]
    weight_ref = refs[8]
    outs = refs[9:11]
    me = read_me(me_ref)
    rows = outs[0].shape[0]
    for side in range(2):
        start = pl.multiple_of(((me["y"] & 1) ^ side) * rows, 128)
        total = None
        for dy in range(4):
            for dc in range(2):
                y = (me["y"] - dy + 4) & 3
                head = 2 * ((y // 2) * 2 + (me["core"] ^ dc)) + (y & 1)
                term = lax.dot_general(
                    attended[2 * dy + dc][pl.ds(start, rows), :],
                    weight_ref[:, pl.ds(pl.multiple_of(head * 256, 256), 256)],
                    (((1,), (1,)), ((), ())),
                    preferred_element_type=F32,
                )
                total = term if total is None else total + term
        outs[side][...] = total.astype(BF16)


def logits_kernel(me_ref, *refs):
    hidden_refs = refs[:4]
    piece_refs = refs[4:12]
    post_ref, final_ref, targets_ref, head_ref, layer_ref, stats_ref = refs[12:18]
    pieces, layers, rows_all, heads, top, total, picked, piece_sem, head_sem = refs[18:]
    me = read_me(me_ref)
    tp = (me["y"] // 2) * 2 + me["core"]
    tokens, width = layer_ref.shape
    count = width * 4
    depth, block, _ = heads.shape
    steps = head_ref.shape[0] // block

    def fetch(step, slot):
        start = pl.multiple_of(step * block, block)
        return pltpu.make_async_copy(head_ref.at[pl.ds(start, block), :], heads.at[slot], head_sem.at[slot])

    copies = []
    for dy in range(4):
        for dc in range(2):
            copies.append(
                pltpu.make_async_copy(
                    piece_refs[2 * dy + dc],
                    pieces.at[(me["y"] - dy + 4) & 3, me["core"] ^ dc],
                    piece_sem.at[2 * dy + dc],
                )
            )
    for copy in copies:
        copy.start()
    for i, ref in enumerate(hidden_refs):
        layers[tp ^ ((0, 2, 1, 3)[i])] = ref[...]
    for copy in copies:
        copy.wait()
    for step in range(depth):
        fetch(step, step).start()

    square = jnp.zeros((tokens, 1), F32)
    for y in range(4):
        for core in range(2):
            piece = pieces[y, core].astype(F32)
            square += jnp.sum(piece * piece, axis=1, keepdims=True)
    scale = lax.rsqrt(square * (1.0 / count) + EPS)
    square = jnp.zeros((tokens, 1), F32)
    for y in range(4):
        joined = jnp.concatenate([pieces[y, 0].astype(F32), pieces[y, 1].astype(F32)], axis=1)
        layer = (layers[y].astype(F32) + joined * scale * post_ref[y]).astype(BF16)
        layers[y] = layer
        wide = layer.astype(F32)
        square += jnp.sum(wide * wide, axis=1, keepdims=True)
    layer_ref[...] = layers[tp]
    scale = lax.rsqrt(square * (1.0 / count) + EPS)
    for y in range(4):
        rows_all[:, pl.ds(y * width, width)] = (layers[y].astype(F32) * scale * final_ref[y]).astype(BF16)

    top[...] = jnp.full_like(top, -jnp.inf)
    total[...] = jnp.zeros_like(total)
    picked[...] = jnp.zeros_like(picked)

    @pl.loop(0, steps)
    def _(step):
        slot = lax.rem(step, depth)
        fetch(step, slot).wait()
        logits = lax.dot_general(
            rows_all[...], heads[slot], (((1,), (1,)), ((), ())), preferred_element_type=F32
        )

        @pl.when(step + depth < steps)
        def _():
            fetch(step + depth, slot).start()

        before = top[...]
        now = jnp.maximum(before, jnp.max(logits, axis=1, keepdims=True))
        top[...] = now
        total[...] = total[...] * jnp.exp(before - now) + jnp.sum(
            jnp.exp(logits - now[:, :1]), axis=1, keepdims=True
        )
        first = (tp * steps + step) * block
        index = first + lax.broadcasted_iota(I32, (1, block), 1)
        picked[...] += jnp.sum(jnp.where(index == targets_ref[...], logits, 0.0), axis=1, keepdims=True)

    lane = lax.broadcasted_iota(I32, top.shape, 1)
    stats = jnp.where(lane == 0, top[...], jnp.where(lane == 1, total[...], picked[...]))
    stats_ref[...] = stats.T[:8]


def params(mib, **extra):
    return pltpu.CompilerParams(vmem_limit_bytes=mib * MIB, **extra)


SMEM = pl.BlockSpec(memory_space=pltpu.SMEM)
VMEM = pl.BlockSpec(memory_space=pltpu.VMEM)
ANY = pl.BlockSpec(memory_space=pl.ANY)


def on_device(
    hidden, attn_gain, w_query, w_key, w_value, w_out, q_gain, k_gain, post_gain, final_gain, lm_head, targets, positions
):
    rows, width = hidden.shape
    tokens = 2 * rows
    quarter = rows // 2
    half = lax.axis_index("yl")
    z, x, core = lax.axis_index("z"), lax.axis_index("x"), lax.axis_index("core")
    y = 2 * lax.axis_index("yh") + half
    me = jnp.stack([z, x, y, core]).astype(I32)

    def both_halves(own, received, axis):
        return jnp.where(
            half == 0, jnp.concatenate([own, received], axis), jnp.concatenate([received, own], axis)
        )

    def columns_of(side):
        return jnp.concatenate(
            [
                lax.dynamic_slice_in_dim(w_query, side * 256, 256, 1),
                lax.dynamic_slice_in_dim(w_key, side * 128, 128, 1),
                lax.dynamic_slice_in_dim(w_value, side * 128, 128, 1),
            ],
            axis=1,
        )

    other_weights = other_half(columns_of(1 - half))
    other_positions = other_half(positions)
    weights = both_halves(columns_of(half), other_weights, 0)

    key_weights = lax.all_gather(weights[:, 256:], ("z", "x"), axis=0, tiled=True)
    ring = [hidden]
    for _ in range(3):
        ring.append(turn(ring[-1], "y"))
    swapped = [other_core(block) for block in ring]
    query_weights = plane_gather([weights[:, 128 * p : 128 * p + 128] for p in range(2)], 0)

    out_rows = send(
        w_out.T,
        lambda place: {
            "z": place["y"],
            "x": 2 * place["core"] + place["x"] % 2,
            "y": place["z"],
            "core": place["x"] // 2,
        },
    )
    out_rows = lax.all_gather(out_rows, ("z", "x"), axis=0)
    feats = out_rows.shape[1]
    out_rows = out_rows.reshape(2, 2, 2, 2, feats, 512).transpose(3, 1, 4, 0, 2, 5).reshape(4 * feats, 2048)

    places = both_halves(positions, other_positions, 0)
    token = (z * 4 + x) * tokens + jnp.arange(tokens, dtype=I32)
    low = jnp.maximum(token - places, 0)
    exponent = jnp.arange(64, dtype=F32) * (2.0 / 128)
    freqs = jnp.exp(-exponent * jnp.log(F32(1000000.0)))
    angles = (places.astype(F32) / 8.0)[:, None] * freqs[None, :]
    cosine, sine = jnp.cos(angles), jnp.sin(angles)
    cosine = jnp.concatenate([cosine, cosine], axis=1)
    sine = jnp.concatenate([-sine, sine], axis=1)

    gain4 = attn_gain.reshape(4, 1, width)
    kv, squares = pl.pallas_call(
        keys_kernel,
        out_shape=(jax.ShapeDtypeStruct((2, 2, rows, 128), BF16), jax.ShapeDtypeStruct((2, rows, 128), F32)),
        in_specs=[SMEM] + [VMEM] * 8 + [ANY] + [VMEM] * 4,
        out_specs=(VMEM, VMEM),
        scratch_shapes=[
            pltpu.VMEM((4 * width, 256), BF16),
            pltpu.VMEM((2, rows, 256), F32),
            pltpu.SemaphoreType.DMA,
        ],
        compiler_params=params(40),
        cost_estimate=pl.CostEstimate(flops=2200000000, bytes_accessed=12000000, transcendentals=0),
        name="keys",
    )(me, *ring, *swapped, key_weights, gain4, k_gain.reshape(1, 128), cosine, sine)
    queries = pl.pallas_call(
        queries_kernel,
        out_shape=jax.ShapeDtypeStruct((2, tokens, 128), BF16),
        in_specs=[SMEM] + [VMEM] * 21,
        out_specs=VMEM,
        scratch_shapes=[
            pltpu.VMEM((4 * width, 256), BF16),
            pltpu.VMEM((2, rows, 256), F32),
            pltpu.SemaphoreType.DMA((32,)),
        ],
        compiler_params=params(40),
        cost_estimate=pl.CostEstimate(flops=2200000000, bytes_accessed=12000000, transcendentals=0),
        name="queries",
    )(
        me,
        *ring,
        *swapped,
        *[block for plane in query_weights for block in plane],
        gain4,
        q_gain.reshape(1, 128),
        cosine,
        sine,
        squares,
    )
    queries = queries.reshape(2 * tokens, 128)

    chunks = plane_gather([kv[1, :, :quarter], kv[1, :, quarter:]], 1)
    firsts, out_rows = lax.optimization_barrier((kv[0], out_rows))
    firsts = lax.all_gather(firsts, ("z", "x"), axis=0)
    edges = low.reshape(-1, 256)
    edges = jnp.stack([edges[:, 0], edges[:, -1]], axis=1).reshape(-1)
    low_col = low.reshape(tokens, 1)
    state = ()
    state_shape = (
        jax.ShapeDtypeStruct((2 * tokens, 128), F32),
        jax.ShapeDtypeStruct((2 * tokens, 256), F32),
    )
    for turn_index, far in enumerate((0, 1, None, 2, 3)):
        first, last = turn_index == 0, turn_index == 4
        sets = [firsts] if far is None else [chunks[p][far] for p in range(2)]
        call = pl.pallas_call(
            functools.partial(attend_kernel, first, last, far),
            out_shape=jax.ShapeDtypeStruct((tokens, 256), BF16) if last else state_shape,
            in_specs=[SMEM, SMEM] + [VMEM] * (2 + len(sets) + len(state)),
            out_specs=VMEM if last else (VMEM, VMEM),
            scratch_shapes=(
                [pltpu.VMEM((2 * tokens, 128), F32), pltpu.VMEM((2 * tokens, 256), F32)] if last else []
            )
            + [pltpu.VMEM((tokens, 256), BF16)],
            compiler_params=params(32),
            cost_estimate=pl.CostEstimate(
                flops=len(sets) * 2400000000, bytes_accessed=8000000, transcendentals=2400000 * len(sets)
            ),
            name=f"attend{turn_index}",
        )
        state = call(me, edges, queries, low_col, *sets, *state)
    attended = state

    column = []
    for dy in range(4):
        block = shift(attended, "y", dy) if dy else attended
        column += [block, other_core(block)]
    same, across = pl.pallas_call(
        project_kernel,
        out_shape=[jax.ShapeDtypeStruct((rows, width // 2), BF16)] * 2,
        in_specs=[SMEM] + [VMEM] * 9,
        out_specs=[VMEM] * 2,
        compiler_params=params(32),
        cost_estimate=pl.CostEstimate(flops=2100000000, bytes_accessed=7000000, transcendentals=0),
        name="project",
    )(me, *column, out_rows)

    pieces = []
    for dy in range(4):
        block = same if dy == 0 else shift(across if dy % 2 else same, "y", dy)
        pieces += [block, other_core(block)]

    block = 256
    layer_out, stats = pl.pallas_call(
        logits_kernel,
        out_shape=(jax.ShapeDtypeStruct((rows, width), BF16), jax.ShapeDtypeStruct((8, rows), F32)),
        in_specs=[SMEM] + [VMEM] * 15 + [ANY],
        out_specs=(VMEM, VMEM),
        scratch_shapes=[
            pltpu.VMEM((4, 2, rows, width // 2), BF16),
            pltpu.VMEM((4, rows, width), BF16),
            pltpu.VMEM((rows, 4 * width), BF16),
            pltpu.VMEM((3, block, 4 * width), BF16),
            pltpu.VMEM((rows, 128), F32),
            pltpu.VMEM((rows, 128), F32),
            pltpu.VMEM((rows, 128), F32),
            pltpu.SemaphoreType.DMA((8,)),
            pltpu.SemaphoreType.DMA((3,)),
        ],
        compiler_params=params(48),
        cost_estimate=pl.CostEstimate(flops=8500000000, bytes_accessed=32000000, transcendentals=800000),
        name="logits",
    )(
        me,
        ring[0],
        ring[2],
        swapped[0],
        swapped[2],
        *pieces,
        post_gain.reshape(4, 1, width),
        final_gain.reshape(4, 1, width),
        targets.reshape(rows, 1),
        lm_head,
    )
    shared = lax.all_gather(stats[:3], ("yh", "core")).transpose(0, 2, 1)
    largest = jnp.max(shared[:, :, 0], axis=0)
    total = jnp.sum(shared[:, :, 1] * jnp.exp(shared[:, :, 0] - largest), axis=0)
    target_logit = jnp.sum(shared[:, :, 2], axis=0)
    logprobs = target_logit - largest - jnp.log(total)
    return (logprobs, layer_out)


def solution(mesh):
    ctx, tp = AXES[:3], AXES[3:]
    return jax.shard_map(
        on_device,
        mesh=Mesh(mesh.devices.reshape(SIZES), AXES),
        in_specs=(
            P(ctx, tp),
            P(),
            P(ctx, tp),
            P(ctx, tp),
            P(ctx, tp),
            P(tp, ctx),
            P(),
            P(),
            P(),
            P(),
            P(tp, None),
            P(ctx),
            P(ctx),
        ),
        out_specs=(P(ctx), P(ctx, tp)),
        check_vma=False,
    )
```

```python
import functools
import math

import jax
import jax.numpy as jnp
from jax import lax
from jax.experimental import pallas as pl
from jax.experimental.pallas import tpu as pltpu
from jax.sharding import Mesh
from jax.sharding import PartitionSpec as P

BF16 = jnp.bfloat16
F32 = jnp.float32
I32 = jnp.int32
EPS = 1e-06
QUERY_SCALE = 168.0 ** (-0.5) * math.log2(math.e)
LOW = -1e30
MIB = 1024 * 1024

PLANS = (("z", "x"), ("x", "z"))
AXES = ("z", "x", "yl", "yh", "core")
SIZES = (4, 4, 2, 2, 2)


def place_of(device):
    place = {}
    for axis, size in zip(reversed(AXES), reversed(SIZES)):
        device, place[axis] = divmod(device, size)
    place["y"] = 2 * place["yh"] + place["yl"]
    return place


def device_of(place):
    y = place["y"] % 4
    place = {**place, "yh": y // 2, "yl": y % 2}
    device = 0
    for axis, size in zip(AXES, SIZES):
        device = device * size + place[axis] % size
    return device


def send(value, move):
    pairs = []
    for device in range(128):
        place = place_of(device)
        pairs.append((device, device_of({**place, **move(place)})))
    return lax.ppermute(value, AXES, pairs)


def shift(value, axis, step):
    return send(value, lambda place: {axis: place[axis] + step})


def other_core(value):
    return shift(value, "core", 1)


def other_half(value):
    return send(value, lambda place: {"y": place["y"] ^ 1})


def around(value, axis):
    return [value] + [shift(value, axis, step) for step in (1, 3, 2)]


BACK = (0, 1, 3, 2)


def plane_gather(parts, axis):
    rows = [jnp.concatenate(around(part, plan[0]), axis=axis) for part, plan in zip(parts, PLANS)]
    return [around(row, plan[1]) for row, plan in zip(rows, PLANS)]


def source(me, plan, far, near):
    at = {plan[0]: (me[plan[0]] - BACK[near] + 4) & 3, plan[1]: (me[plan[1]] - BACK[far] + 4) & 3}
    return at["z"], at["x"]


def read_me(me_ref):
    return {"z": me_ref[0], "x": me_ref[1], "y": me_ref[2], "core": me_ref[3]}


def column_of(me, i):
    return (me["y"] - BACK[i // 2] + 4) & 3, me["core"] ^ (i % 2)


def prepare_kernel(weight_ref, gain_ref, out_ref):
    depth = out_ref.shape[2]

    @pl.loop(0, 4)
    def _(group):
        start = pl.multiple_of(group * depth, 64)
        for piece in range(2):
            cut = pl.ds(256 * piece, 256)
            scaled = weight_ref[pl.ds(start, depth), cut].astype(F32) * gain_ref[pl.ds(start, depth), :]
            out_ref[group, cut, :] = scaled.astype(BF16).T


def normalize(value, gain):
    mean_sq = jnp.mean(value * value, axis=0, keepdims=True)
    return value * lax.rsqrt(mean_sq + EPS) * gain


def project_in_kernel(me_ref, *refs):
    blocks = refs[:8]
    weight_ref, q_gain_ref, k_gain_ref, cos_ref, sin_ref, q_ref, kv_ref = refs[8:15]
    total, squares = refs[15:]
    me = read_me(me_ref)
    depth, rows = blocks[0].shape
    total[...] = jnp.zeros_like(total)
    squares[...] = jnp.zeros_like(squares)
    for i in range(8):
        y, core = column_of(me, i)
        half = y & 1
        block = blocks[i][...]
        wide = block.astype(F32)
        squares[half] += jnp.broadcast_to(jnp.sum(wide * wide, axis=0, keepdims=True), squares.shape[1:])
        total[half] += jnp.dot(weight_ref[(y // 2) * 2 + core], block, preferred_element_type=F32)
    for half in range(2):
        scale = lax.rsqrt(squares[half, :1] * (1.0 / (4 * depth)) + EPS)
        cosine, sine = cos_ref[half], sin_ref[half]

        def head(begin, gain):
            value = normalize(total[half, pl.ds(begin, 128), :] * scale, gain)
            upper, lower = value[:64], value[64:]
            return jnp.concatenate([upper * cosine - lower * sine, lower * cosine + upper * sine], axis=0)

        cut = pl.ds(half * rows, rows)
        for i in range(2):
            q_ref[i, cut, :] = (head(128 * i, q_gain_ref[...]) * QUERY_SCALE).T.astype(BF16)
        kv_ref[0, cut, :] = head(256, k_gain_ref[...]).T.astype(BF16)
        kv_ref[1, cut, :] = (total[half, pl.ds(384, 128), :] * scale).T.astype(BF16)


def attend_kernel(first, last, fars, me_ref, low_ref, q_ref, low_col, *refs):
    count = 2 * len(fars)
    kvs, refs = refs[:count], refs[count:]
    if first:
        refs = (None, None) + refs
    top_in, total_in, *refs = refs
    if last:
        out_ref, top, total, wide = refs
    else:
        top, total, wide = refs
    if first:
        top[...] = jnp.full_like(top, LOW)
        total[...] = jnp.zeros_like(total)
    else:
        top[...] = top_in[...]
        total[...] = total_in[...]
    me = read_me(me_ref)
    tokens = q_ref.shape[1]
    tile = 256
    length = tokens // 2
    begin = (me["z"] * 4 + me["x"]) * tokens
    wide[:, 128:] = jnp.ones((tokens, 128), BF16)

    for index in range(count):
        far, p = fars[index // 2], index % 2
        for pair in range(2):
            bases = []
            for near in (2 * pair, 2 * pair + 1):
                z, x = source(me, PLANS[p], far, near)
                bases.append((z * 4 + x) * tokens + p * length)
            span = pl.ds(pair * tokens, tokens)
            wide[:, :128] = kvs[index][1, span, :]

            @pl.loop(0, tokens // tile)
            def _(piece):
                token = pl.multiple_of(piece * tile, tile)
                q_first = begin + token
                q_last = q_first + tile - 1
                low_first = low_ref[2 * piece]
                low_last = low_ref[2 * piece + 1]
                seen = [(b <= q_last) & (b + length - 1 >= low_first) for b in bases]
                whole = [(b + length - 1 <= q_first) & (b >= low_last) for b in bases]
                some = seen[0] | seen[1]
                every = whole[0] & whole[1]

                def work(masked):
                    keys = kvs[index][0, span, :]
                    rows = pl.ds(token, tile)
                    scores = [
                        lax.dot_general(
                            q_ref[head, rows, :], keys, (((1,), (1,)), ((), ())), preferred_element_type=F32
                        )
                        for head in range(2)
                    ]
                    if masked:
                        lane = lax.broadcasted_iota(I32, (1, tokens), 1)
                        at = jnp.where(lane >= length, bases[1] - length, bases[0]) + lane
                        own = q_first + lax.broadcasted_iota(I32, (tile, 1), 0)
                        visible = (at <= own) & (at >= low_col[rows, :])
                        scores = [jnp.where(visible, score, LOW) for score in scores]
                    for head in range(2):
                        before = top[head, rows, :]
                        now = jnp.maximum(before, jnp.max(scores[head], axis=1, keepdims=True))
                        probs = jnp.exp2(scores[head] - jnp.concatenate([now] * (tokens // 128), axis=1))
                        fade = jnp.exp2(before - now)
                        top[head, rows, :] = now
                        total[head, rows, :] = total[head, rows, :] * jnp.concatenate([fade, fade], axis=1) + jnp.dot(
                            probs.astype(BF16), wide[...], preferred_element_type=F32
                        )

                @pl.when(some & every)
                def _():
                    work(False)

                @pl.when(some & jnp.logical_not(every))
                def _():
                    work(True)

    if last:
        for half in range(2):
            rows = pl.ds(half * length, length)
            for head in range(2):
                value = total[head, rows, pl.ds(0, 128)] / total[head, rows, pl.ds(128, 128)]
                out_ref[half, pl.ds(128 * head, 128), :] = value.T.astype(BF16)


def arrange_kernel(block_ref, out_ref):
    feats = block_ref.shape[1]
    for xl in range(2):
        for yh in range(2):
            for core in range(2):
                pair = [block_ref[(2 * yh + yl) * 4 + 2 * core + xl].astype(F32) for yl in range(2)]
                out_ref[pl.ds(2 * feats * xl, 2 * feats), pl.ds((2 * yh + core) * 512, 512)] = jnp.concatenate(
                    pair, axis=0
                ).astype(BF16)


def project_kernel(me_ref, *refs):
    attended = refs[:8]
    weight_ref = refs[8]
    outs = refs[9:11]
    me = read_me(me_ref)
    for side in range(2):
        half = (me["y"] & 1) ^ side
        total = None
        for i in range(8):
            y, core = column_of(me, i)
            head = 2 * ((y // 2) * 2 + core) + (y & 1)
            term = jnp.dot(
                weight_ref[:, pl.ds(pl.multiple_of(head * 256, 256), 256)],
                attended[i][half],
                preferred_element_type=F32,
            )
            total = term if total is None else total + term
        outs[side][...] = total.astype(BF16)


def logits_kernel(me_ref, *refs):
    hidden_refs = refs[:4]
    piece_refs = refs[4:12]
    post_ref, final_ref, targets_ref, head_ref, layer_ref, stats_ref = refs[12:18]
    pieces, layers, rows_all, heads, top, total, picked, head_sem = refs[18:]
    me = read_me(me_ref)
    tp = (me["y"] // 2) * 2 + me["core"]
    width, tokens = layer_ref.shape
    count = width * 4
    depth, block, _ = heads.shape
    steps = head_ref.shape[0] // block

    def fetch(step, slot):
        start = pl.multiple_of(step * block, block)
        return pltpu.make_async_copy(head_ref.at[pl.ds(start, block), :], heads.at[slot], head_sem.at[slot])

    for step in range(depth):
        fetch(step, step).start()
    square = jnp.zeros((1, tokens), F32)
    for i in range(8):
        y, core = column_of(me, i)
        piece = piece_refs[i][...]
        pieces[y, core] = piece
        wide = piece.astype(F32)
        square += jnp.sum(wide * wide, axis=0, keepdims=True)
    for i, ref in enumerate(hidden_refs):
        layers[tp ^ ((0, 1, 2, 3)[i])] = ref[...]
    scale = lax.rsqrt(square * (1.0 / count) + EPS)
    square = jnp.zeros((1, tokens), F32)
    for y in range(4):
        for core in range(2):
            cut = pl.ds(core * (width // 2), width // 2)
            update = pieces[y, core].astype(F32) * scale * post_ref[y, cut, :]
            layer = (layers[y, cut, :].astype(F32) + update).astype(BF16)
            layers[y, cut, :] = layer
            wide = layer.astype(F32)
            square += jnp.sum(wide * wide, axis=0, keepdims=True)
    layer_ref[...] = layers[tp]
    scale = lax.rsqrt(square * (1.0 / count) + EPS)
    for y in range(4):
        rows_all[pl.ds(y * width, width), :] = (layers[y].astype(F32) * scale * final_ref[y]).astype(BF16)

    top[...] = jnp.full_like(top, LOW)
    total[...] = jnp.zeros_like(total)
    picked[...] = jnp.zeros_like(picked)

    @pl.loop(0, steps)
    def _(step):
        slot = lax.rem(step, depth)
        fetch(step, slot).wait()
        logits = jnp.dot(heads[slot], rows_all[...], preferred_element_type=F32)

        @pl.when(step + depth < steps)
        def _():
            fetch(step + depth, slot).start()

        before = top[...]
        now = jnp.maximum(before, jnp.max(logits, axis=0, keepdims=True))
        top[...] = now
        total[...] = total[...] * jnp.exp(before - now) + jnp.sum(
            jnp.exp(logits - now), axis=0, keepdims=True
        )
        first = (tp * steps + step) * block
        index = first + lax.broadcasted_iota(I32, (block, 1), 0)
        picked[...] += jnp.sum(jnp.where(index == targets_ref[...], logits, 0.0), axis=0, keepdims=True)

    stats_ref[...] = jnp.concatenate([top[...], total[...], picked[...], jnp.zeros((5, tokens), F32)], axis=0)


def params(mib, **extra):
    return pltpu.CompilerParams(vmem_limit_bytes=mib * MIB, **extra)


SMEM = pl.BlockSpec(memory_space=pltpu.SMEM)
VMEM = pl.BlockSpec(memory_space=pltpu.VMEM)
ANY = pl.BlockSpec(memory_space=pl.ANY)


def on_device(
    hidden, attn_gain, w_query, w_key, w_value, w_out, q_gain, k_gain, post_gain, final_gain, lm_head, targets, positions
):
    rows, width = hidden.shape
    tokens = 2 * rows
    half = lax.axis_index("yl")
    z, x, core = lax.axis_index("z"), lax.axis_index("x"), lax.axis_index("core")
    y = 2 * lax.axis_index("yh") + half
    me = jnp.stack([z, x, y, core]).astype(I32)

    def both_halves(own, received, axis):
        return jnp.where(
            half == 0, jnp.concatenate([own, received], axis), jnp.concatenate([received, own], axis)
        )

    def columns_of(side):
        return jnp.concatenate(
            [
                lax.dynamic_slice_in_dim(w_query, side * 256, 256, 1),
                lax.dynamic_slice_in_dim(w_key, side * 128, 128, 1),
                lax.dynamic_slice_in_dim(w_value, side * 128, 128, 1),
            ],
            axis=1,
        )

    other_weights = other_half(columns_of(1 - half))
    other_positions = other_half(positions)
    weights = both_halves(columns_of(half), other_weights, 0)

    weights = lax.all_gather(weights, ("z", "x"), axis=0, tiled=True)

    def column_gather(block):
        return [part for one in around(block, "y") for part in (one, other_core(one))]

    blocks = column_gather(hidden.T)

    places = both_halves(positions, other_positions, 0)
    token = (z * 4 + x) * tokens + jnp.arange(tokens, dtype=I32)
    low = jnp.maximum(token - places, 0)
    exponent = jnp.arange(64, dtype=F32) * (2.0 / 128)
    freqs = jnp.exp(-exponent * jnp.log(F32(1000000.0)))
    angles = (places.astype(F32) / 8.0).reshape(2, 1, rows) * freqs[None, :, None]

    prepared = pl.pallas_call(
        prepare_kernel,
        out_shape=jax.ShapeDtypeStruct((4, 512, width), BF16),
        in_specs=[VMEM] * 2,
        out_specs=VMEM,
        compiler_params=params(24),
        cost_estimate=pl.CostEstimate(flops=3000000, bytes_accessed=12000000, transcendentals=0),
        name="prepare",
    )(weights, attn_gain.reshape(4 * width, 1))
    queries, kv = pl.pallas_call(
        project_in_kernel,
        out_shape=(
            jax.ShapeDtypeStruct((2, tokens, 128), BF16),
            jax.ShapeDtypeStruct((2, tokens, 128), BF16),
        ),
        in_specs=[SMEM] + [VMEM] * 13,
        out_specs=(VMEM, VMEM),
        scratch_shapes=[pltpu.VMEM((2, 512, rows), F32), pltpu.VMEM((2, 8, rows), F32)],
        compiler_params=params(24),
        cost_estimate=pl.CostEstimate(flops=4300000000, bytes_accessed=16000000, transcendentals=0),
        name="project_in",
    )(
        me, *blocks, prepared, q_gain.reshape(128, 1), k_gain.reshape(128, 1), jnp.cos(angles), jnp.sin(angles)
    )

    chunks = plane_gather([kv[:, :rows], kv[:, rows:]], 1)
    edges = low.reshape(-1, 256)
    edges = jnp.stack([edges[:, 0], edges[:, -1]], axis=1).reshape(-1)
    low_col = low.reshape(tokens, 1)
    state = ()
    state_shape = (
        jax.ShapeDtypeStruct((2, tokens, 128), F32),
        jax.ShapeDtypeStruct((2, tokens, 256), F32),
    )
    for turn, fars in enumerate(((0,), (1, 2), (3,))):
        first, last = turn == 0, turn == 2
        sets = [chunks[p][far] for far in fars for p in range(2)]
        call = pl.pallas_call(
            functools.partial(attend_kernel, first, last, fars),
            out_shape=jax.ShapeDtypeStruct((2, 256, rows), BF16) if last else state_shape,
            in_specs=[SMEM, SMEM] + [VMEM] * (2 + len(sets) + len(state)),
            out_specs=VMEM if last else (VMEM, VMEM),
            scratch_shapes=(
                [pltpu.VMEM((2, tokens, 128), F32), pltpu.VMEM((2, tokens, 256), F32)] if last else []
            )
            + [pltpu.VMEM((tokens, 256), BF16)],
            compiler_params=params(32),
            cost_estimate=pl.CostEstimate(
                flops=len(sets) * 2400000000, bytes_accessed=8000000, transcendentals=2400000 * len(sets)
            ),
            name=f"attend{turn}",
        )
        state = call(me, edges, queries, low_col, *sets, *state)
    attended = state

    out_block, _ = lax.optimization_barrier((w_out.T, queries))
    out_block = send(
        out_block,
        lambda place: {
            "z": place["y"],
            "x": 2 * place["core"] + place["x"] % 2,
            "y": place["z"],
            "core": place["x"] // 2,
        },
    )
    feats = out_block.shape[0]
    out_rows = pl.pallas_call(
        arrange_kernel,
        out_shape=jax.ShapeDtypeStruct((4 * feats, 2048), BF16),
        in_specs=[VMEM],
        out_specs=VMEM,
        compiler_params=params(16),
        cost_estimate=pl.CostEstimate(flops=3000000, bytes_accessed=6000000, transcendentals=0),
        name="arrange",
    )(lax.all_gather(out_block, ("z", "x"), axis=0))

    same, across = pl.pallas_call(
        project_kernel,
        out_shape=[jax.ShapeDtypeStruct((width // 2, rows), BF16)] * 2,
        in_specs=[SMEM] + [VMEM] * 9,
        out_specs=[VMEM] * 2,
        compiler_params=params(24),
        cost_estimate=pl.CostEstimate(flops=2100000000, bytes_accessed=7000000, transcendentals=0),
        name="project",
    )(me, *column_gather(attended), out_rows)

    pieces = []
    for dy in BACK:
        block = same if dy == 0 else shift(across if dy % 2 else same, "y", dy)
        pieces += [block, other_core(block)]

    block = 256
    layer_out, stats = pl.pallas_call(
        logits_kernel,
        out_shape=(jax.ShapeDtypeStruct((width, rows), BF16), jax.ShapeDtypeStruct((8, rows), F32)),
        in_specs=[SMEM] + [VMEM] * 15 + [ANY],
        out_specs=(VMEM, VMEM),
        scratch_shapes=[
            pltpu.VMEM((4, 2, width // 2, rows), BF16),
            pltpu.VMEM((4, width, rows), BF16),
            pltpu.VMEM((4 * width, rows), BF16),
            pltpu.VMEM((3, block, 4 * width), BF16),
            pltpu.VMEM((1, rows), F32),
            pltpu.VMEM((1, rows), F32),
            pltpu.VMEM((1, rows), F32),
            pltpu.SemaphoreType.DMA((3,)),
        ],
        compiler_params=params(40),
        cost_estimate=pl.CostEstimate(flops=8500000000, bytes_accessed=32000000, transcendentals=800000),
        name="logits",
    )(
        me,
        blocks[0],
        blocks[1],
        blocks[6],
        blocks[7],
        *pieces,
        post_gain.reshape(4, width, 1),
        final_gain.reshape(4, width, 1),
        targets.reshape(1, rows),
        lm_head,
    )
    shared = lax.all_gather(stats[:3], ("yh", "core"))
    largest = jnp.max(shared[:, 0], axis=0)
    total = jnp.sum(shared[:, 1] * jnp.exp(shared[:, 0] - largest), axis=0)
    target_logit = jnp.sum(shared[:, 2], axis=0)
    logprobs = target_logit - largest - jnp.log(total)
    return (logprobs, layer_out.T)


def solution(mesh):
    ctx, tp = AXES[:3], AXES[3:]
    return jax.shard_map(
        on_device,
        mesh=Mesh(mesh.devices.reshape(SIZES), AXES),
        in_specs=(
            P(ctx, tp),
            P(),
            P(ctx, tp),
            P(ctx, tp),
            P(ctx, tp),
            P(tp, ctx),
            P(),
            P(),
            P(),
            P(),
            P(tp, None),
            P(ctx),
            P(ctx),
        ),
        out_specs=(P(ctx), P(ctx, tp)),
        check_vma=False,
    )
```

```python
import functools
import math

import jax
import jax.numpy as jnp
from jax import lax
from jax.experimental import pallas as pl
from jax.experimental.pallas import tpu as pltpu
from jax.sharding import Mesh
from jax.sharding import PartitionSpec as P

BF16 = jnp.bfloat16
F32 = jnp.float32
I32 = jnp.int32
EPS = 1e-06
QUERY_SCALE = 168.0 ** (-0.5) * math.log2(math.e)
LOW = -1e30
MIB = 1024 * 1024

PLANS = (("z", "x"), ("x", "z"))
AXES = ("z", "x", "yl", "yh", "core")
SIZES = (4, 4, 2, 2, 2)


def place_of(device):
    place = {}
    for axis, size in zip(reversed(AXES), reversed(SIZES)):
        device, place[axis] = divmod(device, size)
    place["y"] = 2 * place["yh"] + place["yl"]
    return place


def device_of(place):
    y = place["y"] % 4
    place = {**place, "yh": y // 2, "yl": y % 2}
    device = 0
    for axis, size in zip(AXES, SIZES):
        device = device * size + place[axis] % size
    return device


def send(value, move):
    pairs = []
    for device in range(128):
        place = place_of(device)
        pairs.append((device, device_of({**place, **move(place)})))
    return lax.ppermute(value, AXES, pairs)


def shift(value, axis, step):
    return send(value, lambda place: {axis: place[axis] + step})


def other_core(value):
    return shift(value, "core", 1)


def other_half(value):
    return send(value, lambda place: {"y": place["y"] ^ 1})


def around(value, axis):
    return [value] + [shift(value, axis, step) for step in (1, 3, 2)]


BACK = (0, 1, 3, 2)


def plane_gather(parts, axis):
    rows = [jnp.concatenate(around(part, plan[0]), axis=axis) for part, plan in zip(parts, PLANS)]
    return [around(row, plan[1]) for row, plan in zip(rows, PLANS)]


def source(me, plan, far, near):
    at = {plan[0]: (me[plan[0]] - BACK[near] + 4) & 3, plan[1]: (me[plan[1]] - BACK[far] + 4) & 3}
    return at["z"], at["x"]


def read_me(me_ref):
    return {"z": me_ref[0], "x": me_ref[1], "y": me_ref[2], "core": me_ref[3]}


def column_of(me, i):
    return (me["y"] - BACK[i // 2] + 4) & 3, me["core"] ^ (i % 2)


def squares_kernel(me_ref, *refs):
    blocks, out_ref = refs[:8], refs[8]
    me = read_me(me_ref)
    out_ref[...] = jnp.zeros_like(out_ref)
    for i in range(8):
        y, _ = column_of(me, i)
        wide = blocks[i][...].astype(F32)
        out_ref[y & 1] += jnp.broadcast_to(jnp.sum(wide * wide, axis=0, keepdims=True), out_ref.shape[1:])


def prepare_kernel(weight_ref, gain_ref, out_ref):
    depth = out_ref.shape[2]

    @pl.loop(0, 4)
    def _(group):
        start = pl.multiple_of(group * depth, 64)
        scaled = weight_ref[pl.ds(start, depth), :].astype(F32) * gain_ref[pl.ds(start, depth), :]
        out_ref[group] = scaled.astype(BF16).T


def prepare_parts_kernel(me_ref, *refs):
    parts, (gain_ref, out_ref, rows) = refs[:8], refs[8:]
    me = read_me(me_ref)
    depth = out_ref.shape[2]
    height = depth // 4
    for p in range(2):
        for far in range(4):
            for near in range(4):
                z, x = source(me, PLANS[p], far, near)
                start = pl.multiple_of((z * 4 + x) * height, 16)
                piece = parts[4 * p + far][pl.ds(near * height, height), :].astype(F32)
                rows[pl.ds(start, height), pl.ds(128 * p, 128)] = (piece * gain_ref[pl.ds(start, height), :]).astype(BF16)

    @pl.loop(0, 4)
    def _(group):
        out_ref[group] = rows[pl.ds(pl.multiple_of(group * depth, 64), depth), :].T


def normalize(value, gain):
    mean_sq = jnp.mean(value * value, axis=0, keepdims=True)
    return value * lax.rsqrt(mean_sq + EPS) * gain


def project_in_kernel(keys, me_ref, *refs):
    blocks = refs[:8]
    weight_ref, squares_ref, gain_ref, cos_ref, sin_ref, out_ref, total = refs[8:]
    me = read_me(me_ref)
    depth, rows = blocks[0].shape
    total[...] = jnp.zeros_like(total)
    for i in range(8):
        y, core = column_of(me, i)
        total[y & 1] += jnp.dot(weight_ref[(y // 2) * 2 + core], blocks[i][...], preferred_element_type=F32)
    for half in range(2):
        scale = lax.rsqrt(squares_ref[half, :1] * (1.0 / (4 * depth)) + EPS)
        cosine, sine = cos_ref[half], sin_ref[half]
        cut = pl.ds(half * rows, rows)
        for i in range(2):
            value = total[half, pl.ds(128 * i, 128), :] * scale
            if i == 0 or not keys:
                value = normalize(value, gain_ref[...])
                upper, lower = value[:64], value[64:]
                value = jnp.concatenate([upper * cosine - lower * sine, lower * cosine + upper * sine], axis=0)
                if not keys:
                    value = value * QUERY_SCALE
            out_ref[i, cut, :] = value.T.astype(BF16)


def attend_kernel(first, last, fars, me_ref, low_ref, q_ref, low_col, *refs):
    count = 2 * len(fars)
    kvs, refs = refs[:count], refs[count:]
    if first:
        refs = (None, None) + refs
    top_in, total_in, *refs = refs
    if last:
        out_ref, top, total, wide = refs
    else:
        top, total, wide = refs
    if first:
        top[...] = jnp.full_like(top, LOW)
        total[...] = jnp.zeros_like(total)
    else:
        top[...] = top_in[...]
        total[...] = total_in[...]
    me = read_me(me_ref)
    tokens = q_ref.shape[1]
    tile = 256
    length = tokens // 2
    begin = (me["z"] * 4 + me["x"]) * tokens
    wide[:, 128:] = jnp.ones((tokens, 128), BF16)

    for index in range(count):
        far, p = fars[index // 2], index % 2
        for pair in range(2):
            bases = []
            for near in (2 * pair, 2 * pair + 1):
                z, x = source(me, PLANS[p], far, near)
                bases.append((z * 4 + x) * tokens + p * length)
            span = pl.ds(pair * tokens, tokens)
            wide[:, :128] = kvs[index][1, span, :]

            @pl.loop(0, tokens // tile)
            def _(piece):
                token = pl.multiple_of(piece * tile, tile)
                q_first = begin + token
                q_last = q_first + tile - 1
                low_first = low_ref[2 * piece]
                low_last = low_ref[2 * piece + 1]
                seen = [(b <= q_last) & (b + length - 1 >= low_first) for b in bases]
                whole = [(b + length - 1 <= q_first) & (b >= low_last) for b in bases]
                some = seen[0] | seen[1]
                every = whole[0] & whole[1]

                def work(masked):
                    keys = kvs[index][0, span, :]
                    rows = pl.ds(token, tile)
                    scores = [
                        lax.dot_general(
                            q_ref[head, rows, :], keys, (((1,), (1,)), ((), ())), preferred_element_type=F32
                        )
                        for head in range(2)
                    ]
                    if masked:
                        lane = lax.broadcasted_iota(I32, (1, tokens), 1)
                        at = jnp.where(lane >= length, bases[1] - length, bases[0]) + lane
                        own = q_first + lax.broadcasted_iota(I32, (tile, 1), 0)
                        visible = (at <= own) & (at >= low_col[rows, :])
                        scores = [jnp.where(visible, score, LOW) for score in scores]
                    for head in range(2):
                        before = top[head, rows, :]
                        now = jnp.maximum(before, jnp.max(scores[head], axis=1, keepdims=True))
                        probs = jnp.exp2(scores[head] - jnp.concatenate([now] * (tokens // 128), axis=1))
                        fade = jnp.exp2(before - now)
                        top[head, rows, :] = now
                        total[head, rows, :] = total[head, rows, :] * jnp.concatenate([fade, fade], axis=1) + jnp.dot(
                            probs.astype(BF16), wide[...], preferred_element_type=F32
                        )

                @pl.when(some & every)
                def _():
                    work(False)

                @pl.when(some & jnp.logical_not(every))
                def _():
                    work(True)

    if last:
        for half in range(2):
            rows = pl.ds(half * length, length)
            for head in range(2):
                value = total[head, rows, pl.ds(0, 128)] / total[head, rows, pl.ds(128, 128)]
                out_ref[half, pl.ds(128 * head, 128), :] = value.T.astype(BF16)


def arrange_kernel(block_ref, out_ref):
    feats = block_ref.shape[1]
    for xl in range(2):
        for yh in range(2):
            for core in range(2):
                pair = [block_ref[(2 * yh + yl) * 4 + 2 * core + xl].astype(F32) for yl in range(2)]
                out_ref[pl.ds(2 * feats * xl, 2 * feats), pl.ds((2 * yh + core) * 512, 512)] = jnp.concatenate(
                    pair, axis=0
                ).astype(BF16)


def project_kernel(me_ref, *refs):
    attended = refs[:8]
    weight_ref = refs[8]
    outs = refs[9:11]
    me = read_me(me_ref)
    for side in range(2):
        half = (me["y"] & 1) ^ side
        total = None
        for i in range(8):
            y, core = column_of(me, i)
            head = 2 * ((y // 2) * 2 + core) + (y & 1)
            term = jnp.dot(
                weight_ref[:, pl.ds(pl.multiple_of(head * 256, 256), 256)],
                attended[i][half],
                preferred_element_type=F32,
            )
            total = term if total is None else total + term
        outs[side][...] = total.astype(BF16)


def logits_kernel(me_ref, *refs):
    hidden_refs = refs[:4]
    piece_refs = refs[4:12]
    post_ref, final_ref, targets_ref, head_ref, layer_ref, stats_ref = refs[12:18]
    rows_all, layers, heads, top, total, picked, head_sem = refs[18:]
    me = read_me(me_ref)
    tp = (me["y"] // 2) * 2 + me["core"]
    width, tokens = layer_ref.shape
    count = width * 4
    depth, block, _ = heads.shape
    steps = head_ref.shape[0] // block

    def fetch(step, slot):
        start = pl.multiple_of(step * block, block)
        return pltpu.make_async_copy(head_ref.at[pl.ds(start, block), :], heads.at[slot], head_sem.at[slot])

    for step in range(depth):
        fetch(step, step).start()
    square = jnp.zeros((1, tokens), F32)
    for i in range(8):
        y, core = column_of(me, i)
        piece = piece_refs[i][...]
        rows_all[pl.ds(pl.multiple_of((2 * y + core) * (width // 2), 16), width // 2), :] = piece
        wide = piece.astype(F32)
        square += jnp.sum(wide * wide, axis=0, keepdims=True)
    for i, ref in enumerate(hidden_refs):
        layers[pl.ds(pl.multiple_of((tp ^ i) * width, 64), width), :] = ref[...]
    scale = lax.rsqrt(square * (1.0 / count) + EPS)
    square = jnp.zeros((1, tokens), F32)
    gains = post_ref[...].T
    for j in range(count // 128):
        cut = pl.ds(128 * j, 128)
        update = rows_all[cut, :].astype(F32) * scale * gains[:, j : j + 1]
        layer = (layers[cut, :].astype(F32) + update).astype(BF16)
        layers[cut, :] = layer
        wide = layer.astype(F32)
        square += jnp.sum(wide * wide, axis=0, keepdims=True)
    layer_ref[...] = layers[pl.ds(pl.multiple_of(tp * width, 64), width), :]
    scale = lax.rsqrt(square * (1.0 / count) + EPS)
    gains = final_ref[...].T
    for j in range(count // 128):
        cut = pl.ds(128 * j, 128)
        rows_all[cut, :] = (layers[cut, :].astype(F32) * scale * gains[:, j : j + 1]).astype(BF16)

    top[...] = jnp.full_like(top, LOW)
    total[...] = jnp.zeros_like(total)
    picked[...] = jnp.zeros_like(picked)

    @pl.loop(0, steps)
    def _(step):
        slot = lax.rem(step, depth)
        fetch(step, slot).wait()
        logits = jnp.dot(heads[slot], rows_all[...], preferred_element_type=F32)

        @pl.when(step + depth < steps)
        def _():
            fetch(step + depth, slot).start()

        before = top[...]
        now = jnp.maximum(before, jnp.max(logits, axis=0, keepdims=True))
        top[...] = now
        total[...] = total[...] * jnp.exp(before - now) + jnp.sum(
            jnp.exp(logits - now), axis=0, keepdims=True
        )
        first = (tp * steps + step) * block
        index = first + lax.broadcasted_iota(I32, (block, 1), 0)
        picked[...] += jnp.sum(jnp.where(index == targets_ref[...], logits, 0.0), axis=0, keepdims=True)

    stats_ref[...] = jnp.concatenate([top[...], total[...], picked[...], jnp.zeros((5, tokens), F32)], axis=0)


def params(mib, **extra):
    return pltpu.CompilerParams(vmem_limit_bytes=mib * MIB, **extra)


SMEM = pl.BlockSpec(memory_space=pltpu.SMEM)
VMEM = pl.BlockSpec(memory_space=pltpu.VMEM)
ANY = pl.BlockSpec(memory_space=pl.ANY)


def on_device(
    hidden, attn_gain, w_query, w_key, w_value, w_out, q_gain, k_gain, post_gain, final_gain, lm_head, targets, positions
):
    rows, width = hidden.shape
    tokens = 2 * rows
    half = lax.axis_index("yl")
    z, x, core = lax.axis_index("z"), lax.axis_index("x"), lax.axis_index("core")
    y = 2 * lax.axis_index("yh") + half
    me = jnp.stack([z, x, y, core]).astype(I32)

    def both_halves(own, received, axis):
        return jnp.where(
            half == 0, jnp.concatenate([own, received], axis), jnp.concatenate([received, own], axis)
        )

    def columns_of(side):
        return jnp.concatenate(
            [
                lax.dynamic_slice_in_dim(w_query, side * 256, 256, 1),
                lax.dynamic_slice_in_dim(w_key, side * 128, 128, 1),
                lax.dynamic_slice_in_dim(w_value, side * 128, 128, 1),
            ],
            axis=1,
        )

    other_weights = other_half(columns_of(1 - half))
    other_positions = other_half(positions)
    weights = both_halves(columns_of(half), other_weights, 0)

    query_weights = lax.all_gather(weights[:, :256], ("z", "x"), axis=0, tiled=True)

    def column_gather(block):
        return [part for one in around(block, "y") for part in (one, other_core(one))]

    blocks = column_gather(hidden.T)
    key_weights = plane_gather([weights[:, 256:384], weights[:, 384:]], 0)
    out_block, _ = lax.optimization_barrier((w_out.T, blocks[2]))
    out_block = send(
        out_block,
        lambda place: {
            "z": place["y"],
            "x": 2 * place["core"] + place["x"] % 2,
            "y": place["z"],
            "core": place["x"] // 2,
        },
    )

    key_weights[0][3], out_block = lax.optimization_barrier((key_weights[0][3], out_block))
    places = both_halves(positions, other_positions, 0)
    token = (z * 4 + x) * tokens + jnp.arange(tokens, dtype=I32)
    low = jnp.maximum(token - places, 0)
    exponent = jnp.arange(64, dtype=F32) * (2.0 / 128)
    freqs = jnp.exp(-exponent * jnp.log(F32(1000000.0)))
    angles = (places.astype(F32) / 8.0).reshape(2, 1, rows) * freqs[None, :, None]

    cosine, sine = jnp.cos(angles), jnp.sin(angles)
    gain_col = attn_gain.reshape(4 * width, 1)
    squares = pl.pallas_call(
        squares_kernel,
        out_shape=jax.ShapeDtypeStruct((2, 8, rows), F32),
        in_specs=[SMEM] + [VMEM] * 8,
        out_specs=VMEM,
        compiler_params=params(16),
        cost_estimate=pl.CostEstimate(flops=8000000, bytes_accessed=8000000, transcendentals=0),
        name="squares",
    )(me, *blocks)

    def project_in(prepared, gain, keys):
        return pl.pallas_call(
            functools.partial(project_in_kernel, keys),
            out_shape=jax.ShapeDtypeStruct((2, tokens, 128), BF16),
            in_specs=[SMEM] + [VMEM] * 13,
            out_specs=VMEM,
            scratch_shapes=[pltpu.VMEM((2, 256, rows), F32)],
            compiler_params=params(24),
            cost_estimate=pl.CostEstimate(flops=2200000000, bytes_accessed=12000000, transcendentals=0),
            name="keys" if keys else "queries",
        )(me, *blocks, prepared, squares, gain.reshape(128, 1), cosine, sine)

    prepare_cost = pl.CostEstimate(flops=3000000, bytes_accessed=6000000, transcendentals=0)
    prepared = pl.pallas_call(
        prepare_parts_kernel,
        out_shape=jax.ShapeDtypeStruct((4, 256, width), BF16),
        in_specs=[SMEM] + [VMEM] * 9,
        out_specs=VMEM,
        scratch_shapes=[pltpu.VMEM((4 * width, 256), BF16)],
        compiler_params=params(24),
        cost_estimate=prepare_cost,
        name="prepare_keys",
    )(me, *key_weights[0], *key_weights[1], gain_col)
    kv = project_in(prepared, k_gain, True)
    prepared = pl.pallas_call(
        prepare_kernel,
        out_shape=jax.ShapeDtypeStruct((4, 256, width), BF16),
        in_specs=[VMEM] * 2,
        out_specs=VMEM,
        compiler_params=params(24),
        cost_estimate=prepare_cost,
        name="prepare_queries",
    )(query_weights, gain_col)
    queries = project_in(prepared, q_gain, False)

    chunks = plane_gather([kv[:, :rows], kv[:, rows:]], 1)
    edges = low.reshape(-1, 256)
    edges = jnp.stack([edges[:, 0], edges[:, -1]], axis=1).reshape(-1)
    low_col = low.reshape(tokens, 1)
    state = ()
    state_shape = (
        jax.ShapeDtypeStruct((2, tokens, 128), F32),
        jax.ShapeDtypeStruct((2, tokens, 256), F32),
    )
    for turn, fars in enumerate(((0,), (1, 2), (3,))):
        first, last = turn == 0, turn == 2
        sets = [chunks[p][far] for far in fars for p in range(2)]
        call = pl.pallas_call(
            functools.partial(attend_kernel, first, last, fars),
            out_shape=jax.ShapeDtypeStruct((2, 256, rows), BF16) if last else state_shape,
            in_specs=[SMEM, SMEM] + [VMEM] * (2 + len(sets) + len(state)),
            out_specs=VMEM if last else (VMEM, VMEM),
            scratch_shapes=(
                [pltpu.VMEM((2, tokens, 128), F32), pltpu.VMEM((2, tokens, 256), F32)] if last else []
            )
            + [pltpu.VMEM((tokens, 256), BF16)],
            compiler_params=params(32),
            cost_estimate=pl.CostEstimate(
                flops=len(sets) * 2400000000, bytes_accessed=8000000, transcendentals=2400000 * len(sets)
            ),
            name=f"attend{turn}",
        )
        state = call(me, edges, queries, low_col, *sets, *state)
    attended = state

    feats = out_block.shape[0]
    out_rows = pl.pallas_call(
        arrange_kernel,
        out_shape=jax.ShapeDtypeStruct((4 * feats, 2048), BF16),
        in_specs=[VMEM],
        out_specs=VMEM,
        compiler_params=params(16),
        cost_estimate=pl.CostEstimate(flops=3000000, bytes_accessed=6000000, transcendentals=0),
        name="arrange",
    )(lax.all_gather(out_block, ("z", "x"), axis=0))

    same, across = pl.pallas_call(
        project_kernel,
        out_shape=[jax.ShapeDtypeStruct((width // 2, rows), BF16)] * 2,
        in_specs=[SMEM] + [VMEM] * 9,
        out_specs=[VMEM] * 2,
        compiler_params=params(24),
        cost_estimate=pl.CostEstimate(flops=2100000000, bytes_accessed=7000000, transcendentals=0),
        name="project",
    )(me, *column_gather(attended), out_rows)

    pieces = []
    for dy in BACK:
        block = same if dy == 0 else shift(across if dy % 2 else same, "y", dy)
        pieces += [block, other_core(block)]

    block = 512

    def table(gain):
        return jnp.pad(gain.reshape(-1, 128), ((0, 128 - 4 * width // 128), (0, 0)))

    layer_out, stats = pl.pallas_call(
        logits_kernel,
        out_shape=(jax.ShapeDtypeStruct((width, rows), BF16), jax.ShapeDtypeStruct((8, rows), F32)),
        in_specs=[SMEM] + [VMEM] * 15 + [ANY],
        out_specs=(VMEM, VMEM),
        scratch_shapes=[
            pltpu.VMEM((4 * width, rows), BF16),
            pltpu.VMEM((4 * width, rows), BF16),
            pltpu.VMEM((2, block, 4 * width), BF16),
            pltpu.VMEM((1, rows), F32),
            pltpu.VMEM((1, rows), F32),
            pltpu.VMEM((1, rows), F32),
            pltpu.SemaphoreType.DMA((2,)),
        ],
        compiler_params=params(40),
        cost_estimate=pl.CostEstimate(flops=8500000000, bytes_accessed=32000000, transcendentals=800000),
        name="logits",
    )(
        me,
        blocks[0],
        blocks[1],
        blocks[6],
        blocks[7],
        *pieces,
        table(post_gain),
        table(final_gain),
        targets.reshape(1, rows),
        lm_head,
    )
    shared = lax.all_gather(stats[:3], ("yh", "core"))
    largest = jnp.max(shared[:, 0], axis=0)
    total = jnp.sum(shared[:, 1] * jnp.exp(shared[:, 0] - largest), axis=0)
    target_logit = jnp.sum(shared[:, 2], axis=0)
    logprobs = target_logit - largest - jnp.log(total)
    return (logprobs, layer_out.T)


def solution(mesh):
    ctx, tp = AXES[:3], AXES[3:]
    return jax.shard_map(
        on_device,
        mesh=Mesh(mesh.devices.reshape(SIZES), AXES),
        in_specs=(
            P(ctx, tp),
            P(),
            P(ctx, tp),
            P(ctx, tp),
            P(ctx, tp),
            P(tp, ctx),
            P(),
            P(),
            P(),
            P(),
            P(tp, None),
            P(ctx),
            P(ctx),
        ),
        out_specs=(P(ctx), P(ctx, tp)),
        check_vma=False,
    )
```

```python
import functools
import math

import jax
import jax.numpy as jnp
from jax import lax
from jax.experimental import pallas as pl
from jax.experimental.pallas import tpu as pltpu
from jax.sharding import Mesh
from jax.sharding import PartitionSpec as P

BF16 = jnp.bfloat16
F32 = jnp.float32
I32 = jnp.int32
EPS = 1e-06
QUERY_SCALE = 168.0 ** (-0.5) * math.log2(math.e)
LOW = -1e30
MIB = 1024 * 1024

PLANS = (("z", "x"), ("x", "z"))
AXES = ("z", "x", "yl", "yh", "core")
SIZES = (4, 4, 2, 2, 2)


def place_of(device):
    place = {}
    for axis, size in zip(reversed(AXES), reversed(SIZES)):
        device, place[axis] = divmod(device, size)
    place["y"] = 2 * place["yh"] + place["yl"]
    return place


def device_of(place):
    y = place["y"] % 4
    place = {**place, "yh": y // 2, "yl": y % 2}
    device = 0
    for axis, size in zip(AXES, SIZES):
        device = device * size + place[axis] % size
    return device


def send(value, move):
    pairs = []
    for device in range(128):
        place = place_of(device)
        pairs.append((device, device_of({**place, **move(place)})))
    return lax.ppermute(value, AXES, pairs)


def shift(value, axis, step):
    return send(value, lambda place: {axis: place[axis] + step})


def other_core(value):
    return shift(value, "core", 1)


def other_half(value):
    return send(value, lambda place: {"y": place["y"] ^ 1})


def around(value, axis):
    return [value] + [shift(value, axis, step) for step in (1, 3, 2)]


BACK = (0, 1, 3, 2)


def plane_gather(parts, axis):
    rows = [jnp.concatenate(around(part, plan[0]), axis=axis) for part, plan in zip(parts, PLANS)]
    return [around(row, plan[1]) for row, plan in zip(rows, PLANS)]


def source(me, plan, far, near):
    at = {plan[0]: (me[plan[0]] - BACK[near] + 4) & 3, plan[1]: (me[plan[1]] - BACK[far] + 4) & 3}
    return at["z"], at["x"]


def read_me(me_ref):
    return {"z": me_ref[0], "x": me_ref[1], "y": me_ref[2], "core": me_ref[3]}


def column_of(me, i):
    return (me["y"] - BACK[i // 2] + 4) & 3, me["core"] ^ (i % 2)


def squares_kernel(me_ref, *refs):
    blocks, out_ref = refs[:8], refs[8]
    me = read_me(me_ref)
    out_ref[...] = jnp.zeros_like(out_ref)
    for i in range(8):
        y, _ = column_of(me, i)
        wide = blocks[i][...].astype(F32)
        out_ref[y & 1] += jnp.broadcast_to(jnp.sum(wide * wide, axis=0, keepdims=True), out_ref.shape[1:])


def prepare_kernel(weight_ref, gain_ref, out_ref):
    depth = out_ref.shape[2]

    @pl.loop(0, 4)
    def _(group):
        start = pl.multiple_of(group * depth, 64)
        for piece in range(2):
            cut = pl.ds(256 * piece, 256)
            scaled = weight_ref[pl.ds(start, depth), cut].astype(F32) * gain_ref[pl.ds(start, depth), :]
            out_ref[group, cut, :] = scaled.astype(BF16).T


def normalize(value, gain):
    mean_sq = jnp.mean(value * value, axis=0, keepdims=True)
    return value * lax.rsqrt(mean_sq + EPS) * gain


def project_in_kernel(me_ref, *refs):
    blocks = refs[:8]
    weight_ref, squares_ref, q_gain_ref, k_gain_ref, cos_ref, sin_ref, q_ref, kv_ref, total = refs[8:]
    me = read_me(me_ref)
    depth, rows = blocks[0].shape
    for i in range(8):
        y, core = column_of(me, i)
        term = jnp.dot(weight_ref[(y // 2) * 2 + core], blocks[i][...], preferred_element_type=F32)
        if i in (0, 2):
            total[y & 1] = term
        else:
            total[y & 1] += term
    for half in range(2):
        scale = lax.rsqrt(squares_ref[half, :1] * (1.0 / (4 * depth)) + EPS)
        cosine, sine = cos_ref[half], sin_ref[half]

        def head(begin, gain):
            value = normalize(total[half, pl.ds(begin, 128), :] * scale, gain)
            upper, lower = value[:64], value[64:]
            return jnp.concatenate([upper * cosine - lower * sine, lower * cosine + upper * sine], axis=0)

        cut = pl.ds(half * rows, rows)
        kv_ref[0, cut, :] = head(256, k_gain_ref[...]).T.astype(BF16)
        kv_ref[1, cut, :] = (total[half, pl.ds(384, 128), :] * scale).T.astype(BF16)
        for i in range(2):
            q_ref[i, cut, :] = (head(128 * i, q_gain_ref[...]) * QUERY_SCALE).T.astype(BF16)


def attend_kernel(first, last, fars, me_ref, low_ref, q_ref, low_col, *refs):
    count = 2 * len(fars)
    kvs, refs = refs[:count], refs[count:]
    if first:
        refs = (None, None) + refs
    top_in, total_in, *refs = refs
    if last:
        out_ref, top, total, wide = refs
    else:
        top, total, wide = refs
    if first:
        top[...] = jnp.full_like(top, LOW)
        total[...] = jnp.zeros_like(total)
    else:
        top[...] = top_in[...]
        total[...] = total_in[...]
    me = read_me(me_ref)
    tokens = q_ref.shape[1]
    tile = 256
    length = tokens // 2
    begin = (me["z"] * 4 + me["x"]) * tokens
    wide[:, 128:] = jnp.ones((tokens, 128), BF16)

    for index in range(count):
        far, p = fars[index // 2], index % 2
        for pair in range(2):
            bases = []
            for near in (2 * pair, 2 * pair + 1):
                z, x = source(me, PLANS[p], far, near)
                bases.append((z * 4 + x) * tokens + p * length)
            span = pl.ds(pair * tokens, tokens)
            wide[:, :128] = kvs[index][1, span, :]

            @pl.loop(0, tokens // tile)
            def _(piece):
                token = pl.multiple_of(piece * tile, tile)
                q_first = begin + token
                q_last = q_first + tile - 1
                low_first = low_ref[2 * piece]
                low_last = low_ref[2 * piece + 1]
                seen = [(b <= q_last) & (b + length - 1 >= low_first) for b in bases]
                whole = [(b + length - 1 <= q_first) & (b >= low_last) for b in bases]
                some = seen[0] | seen[1]
                every = whole[0] & whole[1]

                def work(masked):
                    keys = kvs[index][0, span, :]
                    rows = pl.ds(token, tile)
                    scores = [
                        lax.dot_general(
                            q_ref[head, rows, :], keys, (((1,), (1,)), ((), ())), preferred_element_type=F32
                        )
                        for head in range(2)
                    ]
                    if masked:
                        lane = lax.broadcasted_iota(I32, (1, tokens), 1)
                        at = jnp.where(lane >= length, bases[1] - length, bases[0]) + lane
                        own = q_first + lax.broadcasted_iota(I32, (tile, 1), 0)
                        visible = (at <= own) & (at >= low_col[rows, :])
                        scores = [jnp.where(visible, score, LOW) for score in scores]
                    for head in range(2):
                        before = top[head, rows, :]
                        now = jnp.maximum(before, jnp.max(scores[head], axis=1, keepdims=True))
                        probs = jnp.exp2(scores[head] - jnp.concatenate([now] * (tokens // 128), axis=1))
                        fade = jnp.exp2(before - now)
                        top[head, rows, :] = now
                        total[head, rows, :] = total[head, rows, :] * jnp.concatenate([fade, fade], axis=1) + jnp.dot(
                            probs.astype(BF16), wide[...], preferred_element_type=F32
                        )

                @pl.when(some & every)
                def _():
                    work(False)

                @pl.when(some & jnp.logical_not(every))
                def _():
                    work(True)

    if last:
        for half in range(2):
            rows = pl.ds(half * length, length)
            for head in range(2):
                value = total[head, rows, pl.ds(0, 128)] / total[head, rows, pl.ds(128, 128)]
                out_ref[half, pl.ds(128 * head, 128), :] = value.T.astype(BF16)


def arrange_kernel(block_ref, out_ref):
    feats = block_ref.shape[1]
    for xl in range(2):
        for yh in range(2):
            for core in range(2):
                pair = [block_ref[(2 * yh + yl) * 4 + 2 * core + xl].astype(F32) for yl in range(2)]
                out_ref[pl.ds(2 * feats * xl, 2 * feats), pl.ds((2 * yh + core) * 512, 512)] = jnp.concatenate(
                    pair, axis=0
                ).astype(BF16)


def project_kernel(me_ref, *refs):
    attended = refs[:8]
    weight_ref = refs[8]
    outs = refs[9:11]
    me = read_me(me_ref)
    for side in range(2):
        half = (me["y"] & 1) ^ side
        total = None
        for i in range(8):
            y, core = column_of(me, i)
            head = 2 * ((y // 2) * 2 + core) + (y & 1)
            term = jnp.dot(
                weight_ref[:, pl.ds(pl.multiple_of(head * 256, 256), 256)],
                attended[i][half],
                preferred_element_type=F32,
            )
            total = term if total is None else total + term
        outs[side][...] = total.astype(BF16)


def logits_kernel(me_ref, *refs):
    hidden_refs = refs[:4]
    piece_refs = refs[4:12]
    post_ref, final_ref, targets_ref, head_ref, layer_ref, stats_ref = refs[12:18]
    rows_all, layers, heads, top, total, picked, head_sem = refs[18:]
    me = read_me(me_ref)
    tp = (me["y"] // 2) * 2 + me["core"]
    width, tokens = layer_ref.shape
    count = width * 4
    depth, block, _ = heads.shape
    steps = head_ref.shape[0] // block

    def fetch(step, slot):
        start = pl.multiple_of(step * block, block)
        return pltpu.make_async_copy(head_ref.at[pl.ds(start, block), :], heads.at[slot], head_sem.at[slot])

    for step in range(depth):
        fetch(step, step).start()
    square = jnp.zeros((1, tokens), F32)
    for i in range(8):
        y, core = column_of(me, i)
        piece = piece_refs[i][...]
        rows_all[pl.ds(pl.multiple_of((2 * y + core) * (width // 2), 16), width // 2), :] = piece
        wide = piece.astype(F32)
        square += jnp.sum(wide * wide, axis=0, keepdims=True)
    for i, ref in enumerate(hidden_refs):
        layers[pl.ds(pl.multiple_of((tp ^ i) * width, 64), width), :] = ref[...]
    scale = lax.rsqrt(square * (1.0 / count) + EPS)
    square = jnp.zeros((1, tokens), F32)
    gains = post_ref[...].T
    for j in range(count // 128):
        cut = pl.ds(128 * j, 128)
        update = rows_all[cut, :].astype(F32) * scale * gains[:, j : j + 1]
        layer = (layers[cut, :].astype(F32) + update).astype(BF16)
        layers[cut, :] = layer
        wide = layer.astype(F32)
        square += jnp.sum(wide * wide, axis=0, keepdims=True)
    layer_ref[...] = layers[pl.ds(pl.multiple_of(tp * width, 64), width), :]
    scale = lax.rsqrt(square * (1.0 / count) + EPS)
    gains = final_ref[...].T
    for j in range(count // 128):
        cut = pl.ds(128 * j, 128)
        rows_all[cut, :] = (layers[cut, :].astype(F32) * scale * gains[:, j : j + 1]).astype(BF16)

    top[...] = jnp.full_like(top, LOW)
    total[...] = jnp.zeros_like(total)
    picked[...] = jnp.zeros_like(picked)

    @pl.loop(0, steps)
    def _(step):
        slot = lax.rem(step, depth)
        fetch(step, slot).wait()
        logits = jnp.dot(heads[slot], rows_all[...], preferred_element_type=F32)

        @pl.when(step + depth < steps)
        def _():
            fetch(step + depth, slot).start()

        before = top[...]
        now = jnp.maximum(before, jnp.max(logits, axis=0, keepdims=True))
        top[...] = now
        total[...] = total[...] * jnp.exp(before - now) + jnp.sum(
            jnp.exp(logits - now), axis=0, keepdims=True
        )
        first = (tp * steps + step) * block
        index = first + lax.broadcasted_iota(I32, (block, 1), 0)
        picked[...] += jnp.sum(jnp.where(index == targets_ref[...], logits, 0.0), axis=0, keepdims=True)

    stats_ref[...] = jnp.concatenate([top[...], total[...], picked[...], jnp.zeros((5, tokens), F32)], axis=0)


def params(mib, **extra):
    return pltpu.CompilerParams(vmem_limit_bytes=mib * MIB, **extra)


SMEM = pl.BlockSpec(memory_space=pltpu.SMEM)
VMEM = pl.BlockSpec(memory_space=pltpu.VMEM)
ANY = pl.BlockSpec(memory_space=pl.ANY)


def on_device(
    hidden, attn_gain, w_query, w_key, w_value, w_out, q_gain, k_gain, post_gain, final_gain, lm_head, targets, positions
):
    rows, width = hidden.shape
    tokens = 2 * rows
    half = lax.axis_index("yl")
    z, x, core = lax.axis_index("z"), lax.axis_index("x"), lax.axis_index("core")
    y = 2 * lax.axis_index("yh") + half
    me = jnp.stack([z, x, y, core]).astype(I32)

    def both_halves(own, received, axis):
        return jnp.where(
            half == 0, jnp.concatenate([own, received], axis), jnp.concatenate([received, own], axis)
        )

    def columns_of(side):
        return jnp.concatenate(
            [
                lax.dynamic_slice_in_dim(w_query, side * 256, 256, 1),
                lax.dynamic_slice_in_dim(w_key, side * 128, 128, 1),
                lax.dynamic_slice_in_dim(w_value, side * 128, 128, 1),
            ],
            axis=1,
        )

    other_weights = other_half(columns_of(1 - half))
    other_positions = other_half(positions)
    weights = both_halves(columns_of(half), other_weights, 0)

    weights = lax.all_gather(weights, ("z", "x"), axis=0, tiled=True)

    def column_gather(block):
        return [part for one in around(block, "y") for part in (one, other_core(one))]

    hidden, other_positions = lax.optimization_barrier((hidden.T, other_positions))
    blocks = column_gather(hidden)
    out_block, _ = lax.optimization_barrier((w_out.T, blocks[2]))
    out_block = send(
        out_block,
        lambda place: {
            "z": place["y"],
            "x": 2 * place["core"] + place["x"] % 2,
            "y": place["z"],
            "core": place["x"] // 2,
        },
    )

    blocks[7], out_block = lax.optimization_barrier((blocks[7], out_block))
    places = both_halves(positions, other_positions, 0)
    token = (z * 4 + x) * tokens + jnp.arange(tokens, dtype=I32)
    low = jnp.maximum(token - places, 0)
    exponent = jnp.arange(64, dtype=F32) * (2.0 / 128)
    freqs = jnp.exp(-exponent * jnp.log(F32(1000000.0)))
    angles = (places.astype(F32) / 8.0).reshape(2, 1, rows) * freqs[None, :, None]

    cosine, sine = jnp.cos(angles), jnp.sin(angles)
    gain_col = attn_gain.reshape(4 * width, 1)
    squares = pl.pallas_call(
        squares_kernel,
        out_shape=jax.ShapeDtypeStruct((2, 8, rows), F32),
        in_specs=[SMEM] + [VMEM] * 8,
        out_specs=VMEM,
        compiler_params=params(16),
        cost_estimate=pl.CostEstimate(flops=8000000, bytes_accessed=8000000, transcendentals=0),
        name="squares",
    )(me, *blocks)

    prepared = pl.pallas_call(
        prepare_kernel,
        out_shape=jax.ShapeDtypeStruct((4, 512, width), BF16),
        in_specs=[VMEM] * 2,
        out_specs=VMEM,
        compiler_params=params(24),
        cost_estimate=pl.CostEstimate(flops=3000000, bytes_accessed=12000000, transcendentals=0),
        name="prepare",
    )(weights, gain_col)
    queries, kv = pl.pallas_call(
        project_in_kernel,
        out_shape=(
            jax.ShapeDtypeStruct((2, tokens, 128), BF16),
            jax.ShapeDtypeStruct((2, tokens, 128), BF16),
        ),
        in_specs=[SMEM] + [VMEM] * 14,
        out_specs=(VMEM, VMEM),
        scratch_shapes=[pltpu.VMEM((2, 512, rows), F32)],
        compiler_params=params(24),
        cost_estimate=pl.CostEstimate(flops=4300000000, bytes_accessed=16000000, transcendentals=0),
        name="project_in",
    )(me, *blocks, prepared, squares, q_gain.reshape(128, 1), k_gain.reshape(128, 1), cosine, sine)

    chunks = plane_gather([kv[:, :rows], kv[:, rows:]], 1)
    edges = low.reshape(-1, 256)
    edges = jnp.stack([edges[:, 0], edges[:, -1]], axis=1).reshape(-1)
    low_col = low.reshape(tokens, 1)
    state = ()
    state_shape = (
        jax.ShapeDtypeStruct((2, tokens, 128), F32),
        jax.ShapeDtypeStruct((2, tokens, 256), F32),
    )
    for turn, fars in enumerate(((0,), (1, 2), (3,))):
        first, last = turn == 0, turn == 2
        sets = [chunks[p][far] for far in fars for p in range(2)]
        call = pl.pallas_call(
            functools.partial(attend_kernel, first, last, fars),
            out_shape=jax.ShapeDtypeStruct((2, 256, rows), BF16) if last else state_shape,
            in_specs=[SMEM, SMEM] + [VMEM] * (2 + len(sets) + len(state)),
            out_specs=VMEM if last else (VMEM, VMEM),
            scratch_shapes=(
                [pltpu.VMEM((2, tokens, 128), F32), pltpu.VMEM((2, tokens, 256), F32)] if last else []
            )
            + [pltpu.VMEM((tokens, 256), BF16)],
            compiler_params=params(32),
            cost_estimate=pl.CostEstimate(
                flops=len(sets) * 2400000000, bytes_accessed=8000000, transcendentals=2400000 * len(sets)
            ),
            name=f"attend{turn}",
        )
        state = call(me, edges, queries, low_col, *sets, *state)
    attended = state

    feats = out_block.shape[0]
    out_rows = pl.pallas_call(
        arrange_kernel,
        out_shape=jax.ShapeDtypeStruct((4 * feats, 2048), BF16),
        in_specs=[VMEM],
        out_specs=VMEM,
        compiler_params=params(16),
        cost_estimate=pl.CostEstimate(flops=3000000, bytes_accessed=6000000, transcendentals=0),
        name="arrange",
    )(lax.all_gather(out_block, ("z", "x"), axis=0))

    same, across = pl.pallas_call(
        project_kernel,
        out_shape=[jax.ShapeDtypeStruct((width // 2, rows), BF16)] * 2,
        in_specs=[SMEM] + [VMEM] * 9,
        out_specs=[VMEM] * 2,
        compiler_params=params(24),
        cost_estimate=pl.CostEstimate(flops=2100000000, bytes_accessed=7000000, transcendentals=0),
        name="project",
    )(me, *column_gather(attended), out_rows)

    pieces = []
    for dy in BACK:
        block = same if dy == 0 else shift(across if dy % 2 else same, "y", dy)
        pieces += [block, other_core(block)]

    block = 512

    def table(gain):
        return jnp.pad(gain.reshape(-1, 128), ((0, 128 - 4 * width // 128), (0, 0)))

    layer_out, stats = pl.pallas_call(
        logits_kernel,
        out_shape=(jax.ShapeDtypeStruct((width, rows), BF16), jax.ShapeDtypeStruct((8, rows), F32)),
        in_specs=[SMEM] + [VMEM] * 15 + [ANY],
        out_specs=(VMEM, VMEM),
        scratch_shapes=[
            pltpu.VMEM((4 * width, rows), BF16),
            pltpu.VMEM((4 * width, rows), BF16),
            pltpu.VMEM((2, block, 4 * width), BF16),
            pltpu.VMEM((1, rows), F32),
            pltpu.VMEM((1, rows), F32),
            pltpu.VMEM((1, rows), F32),
            pltpu.SemaphoreType.DMA((2,)),
        ],
        compiler_params=params(40),
        cost_estimate=pl.CostEstimate(flops=8500000000, bytes_accessed=32000000, transcendentals=800000),
        name="logits",
    )(
        me,
        blocks[0],
        blocks[1],
        blocks[6],
        blocks[7],
        *pieces,
        table(post_gain),
        table(final_gain),
        targets.reshape(1, rows),
        lm_head,
    )
    shared = lax.all_gather(stats[:3], ("yh", "core"))
    largest = jnp.max(shared[:, 0], axis=0)
    total = jnp.sum(shared[:, 1] * jnp.exp(shared[:, 0] - largest), axis=0)
    target_logit = jnp.sum(shared[:, 2], axis=0)
    logprobs = target_logit - largest - jnp.log(total)
    return (logprobs, layer_out.T)


def solution(mesh):
    ctx, tp = AXES[:3], AXES[3:]
    return jax.shard_map(
        on_device,
        mesh=Mesh(mesh.devices.reshape(SIZES), AXES),
        in_specs=(
            P(ctx, tp),
            P(),
            P(ctx, tp),
            P(ctx, tp),
            P(ctx, tp),
            P(tp, ctx),
            P(),
            P(),
            P(),
            P(),
            P(tp, None),
            P(ctx),
            P(ctx),
        ),
        out_specs=(P(ctx), P(ctx, tp)),
        check_vma=False,
    )
```

```python
import functools
import math

import jax
import jax.numpy as jnp
from jax import lax
from jax.experimental import pallas as pl
from jax.experimental.pallas import tpu as pltpu
from jax.sharding import Mesh
from jax.sharding import PartitionSpec as P

BF16 = jnp.bfloat16
F32 = jnp.float32
I32 = jnp.int32
EPS = 1e-06
QUERY_SCALE = 168.0 ** (-0.5) * math.log2(math.e)
LOW = -1e30
MIB = 1024 * 1024

PLANS = (("z", "x"), ("x", "z"))
AXES = ("z", "x", "yl", "yh", "core")
SIZES = (4, 4, 2, 2, 2)


def place_of(device):
    place = {}
    for axis, size in zip(reversed(AXES), reversed(SIZES)):
        device, place[axis] = divmod(device, size)
    place["y"] = 2 * place["yh"] + place["yl"]
    return place


def device_of(place):
    y = place["y"] % 4
    place = {**place, "yh": y // 2, "yl": y % 2}
    device = 0
    for axis, size in zip(AXES, SIZES):
        device = device * size + place[axis] % size
    return device


def send(value, move):
    pairs = []
    for device in range(128):
        place = place_of(device)
        pairs.append((device, device_of({**place, **move(place)})))
    return lax.ppermute(value, AXES, pairs)


def shift(value, axis, step):
    return send(value, lambda place: {axis: place[axis] + step})


def other_core(value):
    return shift(value, "core", 1)


def other_half(value):
    return send(value, lambda place: {"y": place["y"] ^ 1})


def around(value, axis):
    return [value] + [shift(value, axis, step) for step in (1, 3, 2)]


BACK = (0, 1, 3, 2)


def plane_gather(parts, axis):
    rows = [jnp.concatenate(around(part, plan[0]), axis=axis) for part, plan in zip(parts, PLANS)]
    return [around(row, plan[1]) for row, plan in zip(rows, PLANS)]


def source(me, plan, far, near):
    at = {plan[0]: (me[plan[0]] - BACK[near] + 4) & 3, plan[1]: (me[plan[1]] - BACK[far] + 4) & 3}
    return at["z"], at["x"]


def read_me(me_ref):
    return {"z": me_ref[0], "x": me_ref[1], "y": me_ref[2], "core": me_ref[3]}


def column_of(me, i):
    return (me["y"] - BACK[i // 2] + 4) & 3, me["core"] ^ (i % 2)


def squares_kernel(me_ref, *refs):
    blocks, out_ref = refs[:8], refs[8]
    me = read_me(me_ref)
    out_ref[...] = jnp.zeros_like(out_ref)
    for i in range(8):
        y, _ = column_of(me, i)
        wide = blocks[i][...].astype(F32)
        out_ref[y & 1] += jnp.broadcast_to(jnp.sum(wide * wide, axis=0, keepdims=True), out_ref.shape[1:])


def prepare_kernel(weight_ref, gain_ref, out_ref):
    depth = out_ref.shape[2]

    @pl.loop(0, 4)
    def _(group):
        start = pl.multiple_of(group * depth, 64)
        for piece in range(2):
            cut = pl.ds(256 * piece, 256)
            scaled = weight_ref[pl.ds(start, depth), cut].astype(F32) * gain_ref[pl.ds(start, depth), :]
            out_ref[group, cut, :] = scaled.astype(BF16).T


def normalize(value, gain):
    mean_sq = jnp.mean(value * value, axis=0, keepdims=True)
    return value * lax.rsqrt(mean_sq + EPS) * gain


def project_in_kernel(me_ref, *refs):
    blocks = refs[:8]
    weight_ref, squares_ref, q_gain_ref, k_gain_ref, cos_ref, sin_ref, q_ref, kv_ref, total = refs[8:]
    me = read_me(me_ref)
    depth, rows = blocks[0].shape
    for i in range(8):
        y, core = column_of(me, i)
        term = jnp.dot(weight_ref[(y // 2) * 2 + core], blocks[i][...], preferred_element_type=F32)
        if i in (0, 2):
            total[y & 1] = term
        else:
            total[y & 1] += term
    for half in range(2):
        scale = lax.rsqrt(squares_ref[half, :1] * (1.0 / (4 * depth)) + EPS)
        cosine, sine = cos_ref[half], sin_ref[half]

        def head(begin, gain):
            value = normalize(total[half, pl.ds(begin, 128), :] * scale, gain)
            upper, lower = value[:64], value[64:]
            return jnp.concatenate([upper * cosine - lower * sine, lower * cosine + upper * sine], axis=0)

        cut = pl.ds(half * rows, rows)
        kv_ref[0, cut, :] = head(256, k_gain_ref[...]).T.astype(BF16)
        kv_ref[1, cut, :] = (total[half, pl.ds(384, 128), :] * scale).T.astype(BF16)
        for i in range(2):
            q_ref[i, cut, :] = (head(128 * i, q_gain_ref[...]) * QUERY_SCALE).T.astype(BF16)


def attend_kernel(first, last, fars, me_ref, low_ref, q_ref, low_col, *refs):
    count = 2 * len(fars)
    kvs, refs = refs[:count], refs[count:]
    if first:
        refs = (None, None) + refs
    top_in, total_in, *refs = refs
    if last:
        out_ref, top, total, wide = refs
    else:
        top, total, wide = refs
    if first:
        top[...] = jnp.full_like(top, LOW)
        total[...] = jnp.zeros_like(total)
    else:
        top[...] = top_in[...]
        total[...] = total_in[...]
    me = read_me(me_ref)
    tokens = q_ref.shape[1]
    tile = 256
    length = tokens // 2
    begin = (me["z"] * 4 + me["x"]) * tokens
    wide[:, 128:] = jnp.ones((tokens, 128), BF16)

    for index in range(count):
        far, p = fars[index // 2], index % 2
        for pair in range(2):
            bases = []
            for near in (2 * pair, 2 * pair + 1):
                z, x = source(me, PLANS[p], far, near)
                bases.append((z * 4 + x) * tokens + p * length)
            span = pl.ds(pair * tokens, tokens)
            wide[:, :128] = kvs[index][1, span, :]

            @pl.loop(0, tokens // tile)
            def _(piece):
                token = pl.multiple_of(piece * tile, tile)
                q_first = begin + token
                q_last = q_first + tile - 1
                low_first = low_ref[2 * piece]
                low_last = low_ref[2 * piece + 1]
                seen = [(b <= q_last) & (b + length - 1 >= low_first) for b in bases]
                whole = [(b + length - 1 <= q_first) & (b >= low_last) for b in bases]
                some = seen[0] | seen[1]
                every = whole[0] & whole[1]

                def work(masked):
                    keys = kvs[index][0, span, :]
                    rows = pl.ds(token, tile)
                    scores = [
                        lax.dot_general(
                            q_ref[head, rows, :], keys, (((1,), (1,)), ((), ())), preferred_element_type=F32
                        )
                        for head in range(2)
                    ]
                    if masked:
                        lane = lax.broadcasted_iota(I32, (1, tokens), 1)
                        at = jnp.where(lane >= length, bases[1] - length, bases[0]) + lane
                        own = q_first + lax.broadcasted_iota(I32, (tile, 1), 0)
                        visible = (at <= own) & (at >= low_col[rows, :])
                        scores = [jnp.where(visible, score, LOW) for score in scores]
                    for head in range(2):
                        before = top[head, rows, :]
                        now = jnp.maximum(before, jnp.max(scores[head], axis=1, keepdims=True))
                        probs = jnp.exp2(scores[head] - jnp.concatenate([now] * (tokens // 128), axis=1))
                        fade = jnp.exp2(before - now)
                        top[head, rows, :] = now
                        total[head, rows, :] = total[head, rows, :] * jnp.concatenate([fade, fade], axis=1) + jnp.dot(
                            probs.astype(BF16), wide[...], preferred_element_type=F32
                        )

                @pl.when(some & every)
                def _():
                    work(False)

                @pl.when(some & jnp.logical_not(every))
                def _():
                    work(True)

    if last:
        for half in range(2):
            rows = pl.ds(half * length, length)
            for head in range(2):
                value = total[head, rows, pl.ds(0, 128)] / total[head, rows, pl.ds(128, 128)]
                out_ref[half, pl.ds(128 * head, 128), :] = value.T.astype(BF16)


def arrange_kernel(block_ref, out_ref):
    feats = block_ref.shape[1]
    for xl in range(2):
        for yh in range(2):
            for core in range(2):
                pair = [block_ref[(2 * yh + yl) * 4 + 2 * core + xl].astype(F32) for yl in range(2)]
                out_ref[pl.ds(2 * feats * xl, 2 * feats), pl.ds((2 * yh + core) * 512, 512)] = jnp.concatenate(
                    pair, axis=0
                ).astype(BF16)


def project_kernel(me_ref, *refs):
    attended = refs[:8]
    weight_ref = refs[8]
    outs = refs[9:11]
    me = read_me(me_ref)
    for side in range(2):
        half = (me["y"] & 1) ^ side
        total = None
        for i in range(8):
            y, core = column_of(me, i)
            head = 2 * ((y // 2) * 2 + core) + (y & 1)
            term = jnp.dot(
                weight_ref[:, pl.ds(pl.multiple_of(head * 256, 256), 256)],
                attended[i][half],
                preferred_element_type=F32,
            )
            total = term if total is None else total + term
        outs[side][...] = total.astype(BF16)


def logits_kernel(me_ref, *refs):
    hidden_refs = refs[:4]
    piece_refs = refs[4:12]
    post_ref, final_ref, targets_ref, head_ref, layer_ref, stats_ref = refs[12:18]
    rows_all, layers, heads, top, total, picked, head_sem = refs[18:]
    me = read_me(me_ref)
    tp = (me["y"] // 2) * 2 + me["core"]
    width, tokens = layer_ref.shape
    count = width * 4
    depth, block, _ = heads.shape
    steps = head_ref.shape[0] // block

    def fetch(step, slot):
        start = pl.multiple_of(step * block, block)
        return pltpu.make_async_copy(head_ref.at[pl.ds(start, block), :], heads.at[slot], head_sem.at[slot])

    for step in range(depth):
        fetch(step, step).start()
    square = jnp.zeros((1, tokens), F32)
    for i in range(8):
        y, core = column_of(me, i)
        piece = piece_refs[i][...]
        rows_all[pl.ds(pl.multiple_of((2 * y + core) * (width // 2), 16), width // 2), :] = piece
        wide = piece.astype(F32)
        square += jnp.sum(wide * wide, axis=0, keepdims=True)
    for i, ref in enumerate(hidden_refs):
        layers[pl.ds(pl.multiple_of((tp ^ i) * width, 64), width), :] = ref[...]
    scale = lax.rsqrt(square * (1.0 / count) + EPS)
    square = jnp.zeros((1, tokens), F32)
    gains = post_ref[...].T
    for j in range(count // 128):
        cut = pl.ds(128 * j, 128)
        update = rows_all[cut, :].astype(F32) * scale * gains[:, j : j + 1]
        layer = (layers[cut, :].astype(F32) + update).astype(BF16)
        layers[cut, :] = layer
        wide = layer.astype(F32)
        square += jnp.sum(wide * wide, axis=0, keepdims=True)
    layer_ref[...] = layers[pl.ds(pl.multiple_of(tp * width, 64), width), :]
    scale = lax.rsqrt(square * (1.0 / count) + EPS)
    gains = final_ref[...].T
    for j in range(count // 128):
        cut = pl.ds(128 * j, 128)
        rows_all[cut, :] = (layers[cut, :].astype(F32) * scale * gains[:, j : j + 1]).astype(BF16)

    top[...] = jnp.full_like(top, LOW)
    total[...] = jnp.zeros_like(total)
    picked[...] = jnp.zeros_like(picked)

    @pl.loop(0, steps)
    def _(step):
        slot = lax.rem(step, depth)
        fetch(step, slot).wait()
        logits = jnp.dot(heads[slot], rows_all[...], preferred_element_type=F32)

        @pl.when(step + depth < steps)
        def _():
            fetch(step + depth, slot).start()

        before = top[...]
        now = jnp.maximum(before, jnp.max(logits, axis=0, keepdims=True))
        top[...] = now
        total[...] = total[...] * jnp.exp(before - now) + jnp.sum(
            jnp.exp(logits - now), axis=0, keepdims=True
        )
        first = (tp * steps + step) * block
        index = first + lax.broadcasted_iota(I32, (block, 1), 0)
        picked[...] += jnp.sum(jnp.where(index == targets_ref[...], logits, 0.0), axis=0, keepdims=True)

    stats_ref[...] = jnp.concatenate([top[...], total[...], picked[...], jnp.zeros((5, tokens), F32)], axis=0)


def params(mib, **extra):
    return pltpu.CompilerParams(vmem_limit_bytes=mib * MIB, **extra)


SMEM = pl.BlockSpec(memory_space=pltpu.SMEM)
VMEM = pl.BlockSpec(memory_space=pltpu.VMEM)
ANY = pl.BlockSpec(memory_space=pl.ANY)


def on_device(
    hidden, attn_gain, w_query, w_key, w_value, w_out, q_gain, k_gain, post_gain, final_gain, lm_head, targets, positions
):
    rows, width = hidden.shape
    tokens = 2 * rows
    half = lax.axis_index("yl")
    z, x, core = lax.axis_index("z"), lax.axis_index("x"), lax.axis_index("core")
    y = 2 * lax.axis_index("yh") + half
    me = jnp.stack([z, x, y, core]).astype(I32)

    def both_halves(own, received, axis):
        return jnp.where(
            half == 0, jnp.concatenate([own, received], axis), jnp.concatenate([received, own], axis)
        )

    def columns_of(side):
        return jnp.concatenate(
            [
                lax.dynamic_slice_in_dim(w_query, side * 256, 256, 1),
                lax.dynamic_slice_in_dim(w_key, side * 128, 128, 1),
                lax.dynamic_slice_in_dim(w_value, side * 128, 128, 1),
            ],
            axis=1,
        )

    other_weights = other_half(columns_of(1 - half))
    other_positions = other_half(positions)
    weights = both_halves(columns_of(half), other_weights, 0)

    weights = lax.all_gather(weights, ("z", "x"), axis=0, tiled=True)

    def column_gather(block):
        return [part for one in around(block, "y") for part in (one, other_core(one))]

    hidden, other_positions = lax.optimization_barrier((hidden.T, other_positions))
    blocks = column_gather(hidden)
    out_block, _ = lax.optimization_barrier((w_out.T, blocks[2]))
    out_block = send(
        out_block,
        lambda place: {
            "z": place["y"],
            "x": 2 * place["core"] + place["x"] % 2,
            "y": place["z"],
            "core": place["x"] // 2,
        },
    )

    places = both_halves(positions, other_positions, 0)
    token = (z * 4 + x) * tokens + jnp.arange(tokens, dtype=I32)
    low = jnp.maximum(token - places, 0)
    exponent = jnp.arange(64, dtype=F32) * (2.0 / 128)
    freqs = jnp.exp(-exponent * jnp.log(F32(1000000.0)))
    angles = (places.astype(F32) / 8.0).reshape(2, 1, rows) * freqs[None, :, None]

    cosine, sine = jnp.cos(angles), jnp.sin(angles)
    gain_col = attn_gain.reshape(4 * width, 1)
    squares = pl.pallas_call(
        squares_kernel,
        out_shape=jax.ShapeDtypeStruct((2, 8, rows), F32),
        in_specs=[SMEM] + [VMEM] * 8,
        out_specs=VMEM,
        compiler_params=params(16),
        cost_estimate=pl.CostEstimate(flops=8000000, bytes_accessed=8000000, transcendentals=0),
        name="squares",
    )(me, *blocks)
    squares, out_block = lax.optimization_barrier((squares, out_block))

    prepared = pl.pallas_call(
        prepare_kernel,
        out_shape=jax.ShapeDtypeStruct((4, 512, width), BF16),
        in_specs=[VMEM] * 2,
        out_specs=VMEM,
        compiler_params=params(24),
        cost_estimate=pl.CostEstimate(flops=3000000, bytes_accessed=12000000, transcendentals=0),
        name="prepare",
    )(weights, gain_col)
    queries, kv = pl.pallas_call(
        project_in_kernel,
        out_shape=(
            jax.ShapeDtypeStruct((2, tokens, 128), BF16),
            jax.ShapeDtypeStruct((2, tokens, 128), BF16),
        ),
        in_specs=[SMEM] + [VMEM] * 14,
        out_specs=(VMEM, VMEM),
        scratch_shapes=[pltpu.VMEM((2, 512, rows), F32)],
        compiler_params=params(24),
        cost_estimate=pl.CostEstimate(flops=4300000000, bytes_accessed=16000000, transcendentals=0),
        name="project_in",
    )(me, *blocks, prepared, squares, q_gain.reshape(128, 1), k_gain.reshape(128, 1), cosine, sine)

    chunks = plane_gather([kv[:, :rows], kv[:, rows:]], 1)
    edges = low.reshape(-1, 256)
    edges = jnp.stack([edges[:, 0], edges[:, -1]], axis=1).reshape(-1)
    low_col = low.reshape(tokens, 1)
    state = ()
    state_shape = (
        jax.ShapeDtypeStruct((2, tokens, 128), F32),
        jax.ShapeDtypeStruct((2, tokens, 256), F32),
    )
    for turn, fars in enumerate(((0,), (1,), (2,), (3,))):
        first, last = turn == 0, turn == 3
        sets = [chunks[p][far] for far in fars for p in range(2)]
        call = pl.pallas_call(
            functools.partial(attend_kernel, first, last, fars),
            out_shape=jax.ShapeDtypeStruct((2, 256, rows), BF16) if last else state_shape,
            in_specs=[SMEM, SMEM] + [VMEM] * (2 + len(sets) + len(state)),
            out_specs=VMEM if last else (VMEM, VMEM),
            scratch_shapes=(
                [pltpu.VMEM((2, tokens, 128), F32), pltpu.VMEM((2, tokens, 256), F32)] if last else []
            )
            + [pltpu.VMEM((tokens, 256), BF16)],
            compiler_params=params(32),
            cost_estimate=pl.CostEstimate(
                flops=len(sets) * 2400000000, bytes_accessed=8000000, transcendentals=2400000 * len(sets)
            ),
            name=f"attend{turn}",
        )
        state = call(me, edges, queries, low_col, *sets, *state)
    attended = state

    feats = out_block.shape[0]
    out_rows = pl.pallas_call(
        arrange_kernel,
        out_shape=jax.ShapeDtypeStruct((4 * feats, 2048), BF16),
        in_specs=[VMEM],
        out_specs=VMEM,
        compiler_params=params(16),
        cost_estimate=pl.CostEstimate(flops=3000000, bytes_accessed=6000000, transcendentals=0),
        name="arrange",
    )(lax.all_gather(out_block, ("z", "x"), axis=0))

    same, across = pl.pallas_call(
        project_kernel,
        out_shape=[jax.ShapeDtypeStruct((width // 2, rows), BF16)] * 2,
        in_specs=[SMEM] + [VMEM] * 9,
        out_specs=[VMEM] * 2,
        compiler_params=params(24),
        cost_estimate=pl.CostEstimate(flops=2100000000, bytes_accessed=7000000, transcendentals=0),
        name="project",
    )(me, *column_gather(attended), out_rows)

    pieces = []
    for dy in BACK:
        block = same if dy == 0 else shift(across if dy % 2 else same, "y", dy)
        pieces += [block, other_core(block)]

    block = 512

    def table(gain):
        return jnp.pad(gain.reshape(-1, 128), ((0, 128 - 4 * width // 128), (0, 0)))

    layer_out, stats = pl.pallas_call(
        logits_kernel,
        out_shape=(jax.ShapeDtypeStruct((width, rows), BF16), jax.ShapeDtypeStruct((8, rows), F32)),
        in_specs=[SMEM] + [VMEM] * 15 + [ANY],
        out_specs=(VMEM, VMEM),
        scratch_shapes=[
            pltpu.VMEM((4 * width, rows), BF16),
            pltpu.VMEM((4 * width, rows), BF16),
            pltpu.VMEM((2, block, 4 * width), BF16),
            pltpu.VMEM((1, rows), F32),
            pltpu.VMEM((1, rows), F32),
            pltpu.VMEM((1, rows), F32),
            pltpu.SemaphoreType.DMA((2,)),
        ],
        compiler_params=params(40),
        cost_estimate=pl.CostEstimate(flops=8500000000, bytes_accessed=32000000, transcendentals=800000),
        name="logits",
    )(
        me,
        blocks[0],
        blocks[1],
        blocks[6],
        blocks[7],
        *pieces,
        table(post_gain),
        table(final_gain),
        targets.reshape(1, rows),
        lm_head,
    )
    shared = lax.all_gather(stats[:3], ("yh", "core"))
    largest = jnp.max(shared[:, 0], axis=0)
    total = jnp.sum(shared[:, 1] * jnp.exp(shared[:, 0] - largest), axis=0)
    target_logit = jnp.sum(shared[:, 2], axis=0)
    logprobs = target_logit - largest - jnp.log(total)
    return (logprobs, layer_out.T)


def solution(mesh):
    ctx, tp = AXES[:3], AXES[3:]
    return jax.shard_map(
        on_device,
        mesh=Mesh(mesh.devices.reshape(SIZES), AXES),
        in_specs=(
            P(ctx, tp),
            P(),
            P(ctx, tp),
            P(ctx, tp),
            P(ctx, tp),
            P(tp, ctx),
            P(),
            P(),
            P(),
            P(),
            P(tp, None),
            P(ctx),
            P(ctx),
        ),
        out_specs=(P(ctx), P(ctx, tp)),
        check_vma=False,
    )
```

```python
import functools
import math

import jax
import jax.numpy as jnp
from jax import lax
from jax.experimental import pallas as pl
from jax.experimental.pallas import tpu as pltpu
from jax.sharding import Mesh
from jax.sharding import PartitionSpec as P

BF16 = jnp.bfloat16
F32 = jnp.float32
I32 = jnp.int32
EPS = 1e-06
QUERY_SCALE = 168.0 ** (-0.5) * math.log2(math.e)
LOW = -1e30
MIB = 1024 * 1024

PLANS = (("z", "x"), ("x", "z"))
AXES = ("z", "x", "yl", "yh", "core")
SIZES = (4, 4, 2, 2, 2)


def place_of(device):
    place = {}
    for axis, size in zip(reversed(AXES), reversed(SIZES)):
        device, place[axis] = divmod(device, size)
    place["y"] = 2 * place["yh"] + place["yl"]
    return place


def device_of(place):
    y = place["y"] % 4
    place = {**place, "yh": y // 2, "yl": y % 2}
    device = 0
    for axis, size in zip(AXES, SIZES):
        device = device * size + place[axis] % size
    return device


def send(value, move):
    pairs = []
    for device in range(128):
        place = place_of(device)
        pairs.append((device, device_of({**place, **move(place)})))
    return lax.ppermute(value, AXES, pairs)


def shift(value, axis, step):
    return send(value, lambda place: {axis: place[axis] + step})


def other_core(value):
    return shift(value, "core", 1)


def other_half(value):
    return send(value, lambda place: {"y": place["y"] ^ 1})


def around(value, axis):
    return [value] + [shift(value, axis, step) for step in (1, 3, 2)]


BACK = (0, 1, 3, 2)


def plane_gather(parts, axis):
    rows = [jnp.concatenate(around(part, plan[0]), axis=axis) for part, plan in zip(parts, PLANS)]
    return [around(row, plan[1]) for row, plan in zip(rows, PLANS)]


def source(me, plan, far, near):
    at = {plan[0]: (me[plan[0]] - BACK[near] + 4) & 3, plan[1]: (me[plan[1]] - BACK[far] + 4) & 3}
    return at["z"], at["x"]


def read_me(me_ref):
    return {"z": me_ref[0], "x": me_ref[1], "y": me_ref[2], "core": me_ref[3]}


def column_of(me, i):
    return (me["y"] - BACK[i // 2] + 4) & 3, me["core"] ^ (i % 2)


def squares_kernel(me_ref, *refs):
    blocks, out_ref = refs[:8], refs[8]
    me = read_me(me_ref)
    out_ref[...] = jnp.zeros_like(out_ref)
    for i in range(8):
        y, _ = column_of(me, i)
        wide = blocks[i][...].astype(F32)
        out_ref[y & 1] += jnp.broadcast_to(jnp.sum(wide * wide, axis=0, keepdims=True), out_ref.shape[1:])


def prepare_kernel(weight_ref, gain_ref, out_ref):
    depth = out_ref.shape[2]

    @pl.loop(0, 4)
    def _(group):
        start = pl.multiple_of(group * depth, 64)
        for piece in range(2):
            cut = pl.ds(256 * piece, 256)
            scaled = weight_ref[pl.ds(start, depth), cut].astype(F32) * gain_ref[pl.ds(start, depth), :]
            out_ref[group, cut, :] = scaled.astype(BF16).T


def normalize(value, gain):
    mean_sq = jnp.mean(value * value, axis=0, keepdims=True)
    return value * lax.rsqrt(mean_sq + EPS) * gain


def project_in_kernel(me_ref, *refs):
    blocks = refs[:8]
    weight_ref, squares_ref, q_gain_ref, k_gain_ref, cos_ref, sin_ref, q_ref, kv_ref, total = refs[8:]
    me = read_me(me_ref)
    depth, rows = blocks[0].shape
    for i in range(8):
        y, core = column_of(me, i)
        term = jnp.dot(weight_ref[(y // 2) * 2 + core], blocks[i][...], preferred_element_type=F32)
        if i in (0, 2):
            total[y & 1] = term
        else:
            total[y & 1] += term
    for half in range(2):
        scale = lax.rsqrt(squares_ref[half, :1] * (1.0 / (4 * depth)) + EPS)
        cosine, sine = cos_ref[half], sin_ref[half]

        def head(begin, gain):
            value = normalize(total[half, pl.ds(begin, 128), :] * scale, gain)
            upper, lower = value[:64], value[64:]
            return jnp.concatenate([upper * cosine - lower * sine, lower * cosine + upper * sine], axis=0)

        cut = pl.ds(half * rows, rows)
        kv_ref[0, cut, :] = head(256, k_gain_ref[...]).T.astype(BF16)
        kv_ref[1, cut, :] = (total[half, pl.ds(384, 128), :] * scale).T.astype(BF16)
        for i in range(2):
            q_ref[i, cut, :] = (head(128 * i, q_gain_ref[...]) * QUERY_SCALE).T.astype(BF16)


def attend_kernel(first, last, fars, me_ref, low_ref, q_ref, low_col, *refs):
    count = 2 * len(fars)
    kvs, refs = refs[:count], refs[count:]
    if first:
        refs = (None, None) + refs
    top_in, total_in, *refs = refs
    if last:
        out_ref, top, total, wide = refs
    else:
        top, total, wide = refs
    if first:
        top[...] = jnp.full_like(top, LOW)
        total[...] = jnp.zeros_like(total)
    else:
        top[...] = top_in[...]
        total[...] = total_in[...]
    me = read_me(me_ref)
    tokens = q_ref.shape[1]
    tile = 256
    length = tokens // 2
    begin = (me["z"] * 4 + me["x"]) * tokens
    wide[:, 128:] = jnp.ones((tokens, 128), BF16)

    for index in range(count):
        far, p = fars[index // 2], index % 2
        for pair in range(2):
            bases = []
            for near in (2 * pair, 2 * pair + 1):
                z, x = source(me, PLANS[p], far, near)
                bases.append((z * 4 + x) * tokens + p * length)
            span = pl.ds(pair * tokens, tokens)
            wide[:, :128] = kvs[index][1, span, :]

            @pl.loop(0, tokens // tile)
            def _(piece):
                token = pl.multiple_of(piece * tile, tile)
                q_first = begin + token
                q_last = q_first + tile - 1
                low_first = low_ref[2 * piece]
                low_last = low_ref[2 * piece + 1]
                seen = [(b <= q_last) & (b + length - 1 >= low_first) for b in bases]
                whole = [(b + length - 1 <= q_first) & (b >= low_last) for b in bases]
                some = seen[0] | seen[1]
                every = whole[0] & whole[1]

                def work(masked):
                    keys = kvs[index][0, span, :]
                    rows = pl.ds(token, tile)
                    scores = [
                        lax.dot_general(
                            q_ref[head, rows, :], keys, (((1,), (1,)), ((), ())), preferred_element_type=F32
                        )
                        for head in range(2)
                    ]
                    if masked:
                        lane = lax.broadcasted_iota(I32, (1, tokens), 1)
                        at = jnp.where(lane >= length, bases[1] - length, bases[0]) + lane
                        own = q_first + lax.broadcasted_iota(I32, (tile, 1), 0)
                        visible = (at <= own) & (at >= low_col[rows, :])
                        scores = [jnp.where(visible, score, LOW) for score in scores]
                    for head in range(2):
                        before = top[head, rows, :]
                        now = jnp.maximum(before, jnp.max(scores[head], axis=1, keepdims=True))
                        gap = scores[head] - jnp.concatenate([now] * (tokens // 128), axis=1)
                        probs = jnp.exp2(gap.astype(BF16))
                        fade = jnp.exp2(before - now)
                        top[head, rows, :] = now
                        total[head, rows, :] = total[head, rows, :] * jnp.concatenate([fade, fade], axis=1) + jnp.dot(
                            probs, wide[...], preferred_element_type=F32
                        )

                @pl.when(some & every)
                def _():
                    work(False)

                @pl.when(some & jnp.logical_not(every))
                def _():
                    work(True)

    if last:
        for half in range(2):
            rows = pl.ds(half * length, length)
            for head in range(2):
                value = total[head, rows, pl.ds(0, 128)] / total[head, rows, pl.ds(128, 128)]
                out_ref[half, pl.ds(128 * head, 128), :] = value.T.astype(BF16)


def arrange_kernel(block_ref, out_ref):
    feats = block_ref.shape[1]
    for xl in range(2):
        for yh in range(2):
            for core in range(2):
                pair = [block_ref[(2 * yh + yl) * 4 + 2 * core + xl].astype(F32) for yl in range(2)]
                out_ref[pl.ds(2 * feats * xl, 2 * feats), pl.ds((2 * yh + core) * 512, 512)] = jnp.concatenate(
                    pair, axis=0
                ).astype(BF16)


def project_kernel(me_ref, *refs):
    attended = refs[:8]
    weight_ref = refs[8]
    outs = refs[9:11]
    me = read_me(me_ref)
    for side in range(2):
        half = (me["y"] & 1) ^ side
        total = None
        for i in range(8):
            y, core = column_of(me, i)
            head = 2 * ((y // 2) * 2 + core) + (y & 1)
            term = jnp.dot(
                weight_ref[:, pl.ds(pl.multiple_of(head * 256, 256), 256)],
                attended[i][half],
                preferred_element_type=F32,
            )
            total = term if total is None else total + term
        outs[side][...] = total.astype(BF16)


def logits_kernel(me_ref, *refs):
    hidden_refs = refs[:4]
    piece_refs = refs[4:12]
    post_ref, final_ref, targets_ref, head_ref, layer_ref, stats_ref = refs[12:18]
    rows_all, layers, heads, top, total, picked, head_sem = refs[18:]
    me = read_me(me_ref)
    tp = (me["y"] // 2) * 2 + me["core"]
    width, tokens = layer_ref.shape
    count = width * 4
    depth, block, _ = heads.shape
    steps = head_ref.shape[0] // block

    def fetch(step, slot):
        start = pl.multiple_of(step * block, block)
        return pltpu.make_async_copy(head_ref.at[pl.ds(start, block), :], heads.at[slot], head_sem.at[slot])

    for step in range(depth):
        fetch(step, step).start()
    square = jnp.zeros((1, tokens), F32)
    for i in range(8):
        y, core = column_of(me, i)
        piece = piece_refs[i][...]
        rows_all[pl.ds(pl.multiple_of((2 * y + core) * (width // 2), 16), width // 2), :] = piece
        wide = piece.astype(F32)
        square += jnp.sum(wide * wide, axis=0, keepdims=True)
    for i, ref in enumerate(hidden_refs):
        layers[pl.ds(pl.multiple_of((tp ^ i) * width, 64), width), :] = ref[...]
    scale = lax.rsqrt(square * (1.0 / count) + EPS)
    square = jnp.zeros((1, tokens), F32)
    gains = post_ref[...].T
    for j in range(count // 128):
        cut = pl.ds(128 * j, 128)
        update = rows_all[cut, :].astype(F32) * scale * gains[:, j : j + 1]
        layer = (layers[cut, :].astype(F32) + update).astype(BF16)
        layers[cut, :] = layer
        wide = layer.astype(F32)
        square += jnp.sum(wide * wide, axis=0, keepdims=True)
    layer_ref[...] = layers[pl.ds(pl.multiple_of(tp * width, 64), width), :]
    scale = lax.rsqrt(square * (1.0 / count) + EPS)
    gains = final_ref[...].T
    for j in range(count // 128):
        cut = pl.ds(128 * j, 128)
        rows_all[cut, :] = (layers[cut, :].astype(F32) * scale * gains[:, j : j + 1]).astype(BF16)

    top[...] = jnp.full_like(top, LOW)
    total[...] = jnp.zeros_like(total)
    picked[...] = jnp.zeros_like(picked)

    @pl.loop(0, steps)
    def _(step):
        slot = lax.rem(step, depth)
        fetch(step, slot).wait()
        logits = jnp.dot(heads[slot], rows_all[...], preferred_element_type=F32)

        @pl.when(step + depth < steps)
        def _():
            fetch(step + depth, slot).start()

        before = top[...]
        now = jnp.maximum(before, jnp.max(logits, axis=0, keepdims=True))
        top[...] = now
        total[...] = total[...] * jnp.exp(before - now) + jnp.sum(
            jnp.exp(logits - now), axis=0, keepdims=True
        )
        first = (tp * steps + step) * block
        index = first + lax.broadcasted_iota(I32, (block, 1), 0)
        picked[...] += jnp.sum(jnp.where(index == targets_ref[...], logits, 0.0), axis=0, keepdims=True)

    stats_ref[...] = jnp.concatenate([top[...], total[...], picked[...], jnp.zeros((5, tokens), F32)], axis=0)


def params(mib, **extra):
    return pltpu.CompilerParams(vmem_limit_bytes=mib * MIB, **extra)


SMEM = pl.BlockSpec(memory_space=pltpu.SMEM)
VMEM = pl.BlockSpec(memory_space=pltpu.VMEM)
ANY = pl.BlockSpec(memory_space=pl.ANY)


def on_device(
    hidden, attn_gain, w_query, w_key, w_value, w_out, q_gain, k_gain, post_gain, final_gain, lm_head, targets, positions
):
    rows, width = hidden.shape
    tokens = 2 * rows
    half = lax.axis_index("yl")
    z, x, core = lax.axis_index("z"), lax.axis_index("x"), lax.axis_index("core")
    y = 2 * lax.axis_index("yh") + half
    me = jnp.stack([z, x, y, core]).astype(I32)

    def both_halves(own, received, axis):
        return jnp.where(
            half == 0, jnp.concatenate([own, received], axis), jnp.concatenate([received, own], axis)
        )

    def columns_of(side):
        return jnp.concatenate(
            [
                lax.dynamic_slice_in_dim(w_query, side * 256, 256, 1),
                lax.dynamic_slice_in_dim(w_key, side * 128, 128, 1),
                lax.dynamic_slice_in_dim(w_value, side * 128, 128, 1),
            ],
            axis=1,
        )

    other_weights = other_half(columns_of(1 - half))
    other_positions = other_half(positions)
    weights = both_halves(columns_of(half), other_weights, 0)

    weights = lax.all_gather(weights, ("z", "x"), axis=0, tiled=True)

    def column_gather(block):
        return [part for one in around(block, "y") for part in (one, other_core(one))]

    hidden, other_positions = lax.optimization_barrier((hidden.T, other_positions))
    blocks = column_gather(hidden)
    out_block, _ = lax.optimization_barrier((w_out.T, blocks[2]))
    out_block = send(
        out_block,
        lambda place: {
            "z": place["y"],
            "x": 2 * place["core"] + place["x"] % 2,
            "y": place["z"],
            "core": place["x"] // 2,
        },
    )

    places = both_halves(positions, other_positions, 0)
    token = (z * 4 + x) * tokens + jnp.arange(tokens, dtype=I32)
    low = jnp.maximum(token - places, 0)
    exponent = jnp.arange(64, dtype=F32) * (2.0 / 128)
    freqs = jnp.exp(-exponent * jnp.log(F32(1000000.0)))
    angles = (places.astype(F32) / 8.0).reshape(2, 1, rows) * freqs[None, :, None]

    cosine, sine = jnp.cos(angles), jnp.sin(angles)
    gain_col = attn_gain.reshape(4 * width, 1)
    squares = pl.pallas_call(
        squares_kernel,
        out_shape=jax.ShapeDtypeStruct((2, 8, rows), F32),
        in_specs=[SMEM] + [VMEM] * 8,
        out_specs=VMEM,
        compiler_params=params(16),
        cost_estimate=pl.CostEstimate(flops=8000000, bytes_accessed=8000000, transcendentals=0),
        name="squares",
    )(me, *blocks)
    squares, out_block = lax.optimization_barrier((squares, out_block))

    prepared = pl.pallas_call(
        prepare_kernel,
        out_shape=jax.ShapeDtypeStruct((4, 512, width), BF16),
        in_specs=[VMEM] * 2,
        out_specs=VMEM,
        compiler_params=params(24),
        cost_estimate=pl.CostEstimate(flops=3000000, bytes_accessed=12000000, transcendentals=0),
        name="prepare",
    )(weights, gain_col)
    queries, kv = pl.pallas_call(
        project_in_kernel,
        out_shape=(
            jax.ShapeDtypeStruct((2, tokens, 128), BF16),
            jax.ShapeDtypeStruct((2, tokens, 128), BF16),
        ),
        in_specs=[SMEM] + [VMEM] * 14,
        out_specs=(VMEM, VMEM),
        scratch_shapes=[pltpu.VMEM((2, 512, rows), F32)],
        compiler_params=params(24),
        cost_estimate=pl.CostEstimate(flops=4300000000, bytes_accessed=16000000, transcendentals=0),
        name="project_in",
    )(me, *blocks, prepared, squares, q_gain.reshape(128, 1), k_gain.reshape(128, 1), cosine, sine)

    chunks = plane_gather([kv[:, :rows], kv[:, rows:]], 1)
    edges = low.reshape(-1, 256)
    edges = jnp.stack([edges[:, 0], edges[:, -1]], axis=1).reshape(-1)
    low_col = low.reshape(tokens, 1)
    state = ()
    state_shape = (
        jax.ShapeDtypeStruct((2, tokens, 128), F32),
        jax.ShapeDtypeStruct((2, tokens, 256), F32),
    )
    for turn, fars in enumerate(((0,), (1,), (2,), (3,))):
        first, last = turn == 0, turn == 3
        sets = [chunks[p][far] for far in fars for p in range(2)]
        call = pl.pallas_call(
            functools.partial(attend_kernel, first, last, fars),
            out_shape=jax.ShapeDtypeStruct((2, 256, rows), BF16) if last else state_shape,
            in_specs=[SMEM, SMEM] + [VMEM] * (2 + len(sets) + len(state)),
            out_specs=VMEM if last else (VMEM, VMEM),
            scratch_shapes=(
                [pltpu.VMEM((2, tokens, 128), F32), pltpu.VMEM((2, tokens, 256), F32)] if last else []
            )
            + [pltpu.VMEM((tokens, 256), BF16)],
            compiler_params=params(32),
            cost_estimate=pl.CostEstimate(
                flops=len(sets) * 2400000000, bytes_accessed=8000000, transcendentals=2400000 * len(sets)
            ),
            name=f"attend{turn}",
        )
        state = call(me, edges, queries, low_col, *sets, *state)
    attended = state

    feats = out_block.shape[0]
    out_rows = pl.pallas_call(
        arrange_kernel,
        out_shape=jax.ShapeDtypeStruct((4 * feats, 2048), BF16),
        in_specs=[VMEM],
        out_specs=VMEM,
        compiler_params=params(16),
        cost_estimate=pl.CostEstimate(flops=3000000, bytes_accessed=6000000, transcendentals=0),
        name="arrange",
    )(lax.all_gather(out_block, ("z", "x"), axis=0))

    same, across = pl.pallas_call(
        project_kernel,
        out_shape=[jax.ShapeDtypeStruct((width // 2, rows), BF16)] * 2,
        in_specs=[SMEM] + [VMEM] * 9,
        out_specs=[VMEM] * 2,
        compiler_params=params(24),
        cost_estimate=pl.CostEstimate(flops=2100000000, bytes_accessed=7000000, transcendentals=0),
        name="project",
    )(me, *column_gather(attended), out_rows)

    pieces = []
    for dy in BACK:
        block = same if dy == 0 else shift(across if dy % 2 else same, "y", dy)
        pieces += [block, other_core(block)]

    block = 512

    def table(gain):
        return jnp.pad(gain.reshape(-1, 128), ((0, 128 - 4 * width // 128), (0, 0)))

    layer_out, stats = pl.pallas_call(
        logits_kernel,
        out_shape=(jax.ShapeDtypeStruct((width, rows), BF16), jax.ShapeDtypeStruct((8, rows), F32)),
        in_specs=[SMEM] + [VMEM] * 15 + [ANY],
        out_specs=(VMEM, VMEM),
        scratch_shapes=[
            pltpu.VMEM((4 * width, rows), BF16),
            pltpu.VMEM((4 * width, rows), BF16),
            pltpu.VMEM((2, block, 4 * width), BF16),
            pltpu.VMEM((1, rows), F32),
            pltpu.VMEM((1, rows), F32),
            pltpu.VMEM((1, rows), F32),
            pltpu.SemaphoreType.DMA((2,)),
        ],
        compiler_params=params(40),
        cost_estimate=pl.CostEstimate(flops=8500000000, bytes_accessed=32000000, transcendentals=800000),
        name="logits",
    )(
        me,
        blocks[0],
        blocks[1],
        blocks[6],
        blocks[7],
        *pieces,
        table(post_gain),
        table(final_gain),
        targets.reshape(1, rows),
        lm_head,
    )
    shared = lax.all_gather(stats[:3], ("yh", "core"))
    largest = jnp.max(shared[:, 0], axis=0)
    total = jnp.sum(shared[:, 1] * jnp.exp(shared[:, 0] - largest), axis=0)
    target_logit = jnp.sum(shared[:, 2], axis=0)
    logprobs = target_logit - largest - jnp.log(total)
    return (logprobs, layer_out.T)


def solution(mesh):
    ctx, tp = AXES[:3], AXES[3:]
    return jax.shard_map(
        on_device,
        mesh=Mesh(mesh.devices.reshape(SIZES), AXES),
        in_specs=(
            P(ctx, tp),
            P(),
            P(ctx, tp),
            P(ctx, tp),
            P(ctx, tp),
            P(tp, ctx),
            P(),
            P(),
            P(),
            P(),
            P(tp, None),
            P(ctx),
            P(ctx),
        ),
        out_specs=(P(ctx), P(ctx, tp)),
        check_vma=False,
    )
```
